32 devices in a mesh: parts: 2 (over y), row: 4 (over z), loop: 4 (over x, core).
Axes of the slice: x: 2, y: 2, z: 4, core: 2. Of those that a mesh axis runs over, the one named last changes fastest.
Arguments:
- geometry: float32 [7, 16384], P(None, ('parts', 'row', 'loop')), parts along dimension 1, as said below
- adjoint: float32 [64, 16384], P(None, ('parts', 'row', 'loop')), parts along dimension 1, may hold values from -1.8 to 1.8
- forward: float32 [64, 16384], P(None, ('parts', 'row', 'loop')), parts along dimension 1, may hold values from -1.8 to 1.8
- owner_map: int32 [4, 16384], P(None, ('parts', 'row', 'loop')), parts along dimension 1, may hold values from 0 to 511
- owner_weight: float32 [4, 16384], P(None, ('parts', 'row', 'loop')), parts along dimension 1, may hold values from 0.1 to 1
Outputs:
- shape_gradient: float32 [6, 1024], P(None, ('parts', 'row', 'loop')), parts along dimension 1
The draws below stay inside these ranges and needn't reach their ends.
There are 2 independent parts, one for each index of `parts`. The reference program is written for one: setup_inputs(seed, part) draws one part's arguments, and reference() takes and returns one part's arrays. A program takes and returns all parts, laid end to end along the dimension named above; each array names one. Nothing has to cross between parts.
Inputs may be any that keep to these rules, and one draw needn't show every extreme that they name: Rows 0 to 2 of geometry are centroids in metres on a hull surface, with the axial coordinate (row 0) not falling with the panel number; rows 3 to 5 are its unit outward normals, row 6 areas between 0.004 and 0.04.
All inputs are finite; a program needn't handle non-finite values.
Results may differ from the reference program's by a relative error of at most 0.0003.
Values sent between devices are 32-bit elements; how exact they have to be, the bound alone decides.
No kernel may reach another device: no remote copies, remote signals or barrier semaphores. Data moves between devices by JAX's collectives and lax.ppermute only.
A program may use at most 64 MiB of HBM per device.

```python
import math
import jax
import jax.numpy as jnp
from jax import lax

PAN_DEV = 512
NDIR = 32
OWN = 4
GROUP = 2048
PANELS = 8192
NCP = 512
N_ROW = 4
N_LOOP = 4


def draw_geometry(key, part):
    subkeys = jax.random.split(key, 3)
    half_length = 30.0
    hull_radius = 3.5
    cap_length = 6.0
    jitter = jax.random.uniform(subkeys[0], (PANELS,), jnp.float32, 0.0, 1.0)
    position = jnp.arange(PANELS, dtype=jnp.float32) + jitter
    along = -half_length + 2.0 * half_length * position / PANELS
    angle = jax.random.uniform(subkeys[1], (PANELS,), jnp.float32, -math.pi, math.pi)
    straight_end = half_length - cap_length
    beyond = jnp.maximum(jnp.abs(along) - straight_end, 0.0)
    fraction = jnp.minimum(beyond / cap_length, 1.0)
    local_radius = hull_radius * jnp.sqrt(jnp.maximum(1.0 - fraction * fraction, 0.0))
    cos_angle = jnp.cos(angle)
    sin_angle = jnp.sin(angle)
    axial_part = jnp.sign(along) * fraction / cap_length
    radial_part = local_radius / (hull_radius * hull_radius)
    normal_length = jnp.sqrt(axial_part * axial_part + radial_part * radial_part)
    normals = jnp.stack([axial_part / normal_length, radial_part * cos_angle / normal_length, radial_part * sin_angle / normal_length], axis=0)
    centres = jnp.stack([along, local_radius * cos_angle, local_radius * sin_angle], axis=0)
    log_area = jax.random.uniform(subkeys[2], (1, PANELS), jnp.float32, math.log(0.004), math.log(0.04))
    return jnp.concatenate([centres, normals, jnp.exp(log_area)], axis=0).astype(jnp.float32)


def touch_ends(entries, key, smallest, high):
    index_at = [jax.random.randint(jax.random.fold_in(key, axis), (), 0, length) for axis, length in enumerate(entries.shape)]
    longest = entries.shape.index(max(entries.shape))
    beside = index_at[:longest] + [(index_at[longest] + 1) % entries.shape[longest]] + index_at[longest + 1:]
    return entries.at[tuple(index_at)].set(smallest).at[tuple(beside)].set(high)


def steps_of(own_key, shape, pieces, low, largest):
    factor_of = 1.0
    for dim, shards_of in pieces:
        steps = jax.random.uniform(jax.random.fold_in(jax.random.fold_in(own_key, 6), dim), (shards_of,), jnp.float32, low / len(pieces), largest / len(pieces))
        factor_of = factor_of * jnp.repeat(jnp.exp(steps), shape[dim] // shards_of).reshape((-1,) + (1,) * (len(shape) - 1 - dim))
    return factor_of


def gaussian(rng, extent, scale, most, shards=(), kind=jnp.bfloat16):
    drawn = jax.random.normal(rng, extent, jnp.float32) * scale
    if len(shards) > 0:
        drawn = steps_of(rng, extent, shards, -0.22, 0.18) * drawn
    return jnp.clip(drawn, min=-most, max=most).astype(kind)


def setup_inputs(seed: int = 0, part: int = 0) -> dict:
    keys = jax.random.split(jax.random.key(seed), 6)
    own_keys = jax.random.split(jax.random.fold_in(keys[5], part), 6)
    geometry = draw_geometry(jax.random.fold_in(jax.random.fold_in(keys[5], part), 71), part)
    adjoint = gaussian(own_keys[1], (2 * NDIR, PANELS), 0.3, 1.8, ((1, 16),), jnp.float32)
    forward = gaussian(own_keys[2], (2 * NDIR, PANELS), 0.3, 1.8, ((1, 16),), jnp.float32)
    owner_map = touch_ends(jax.random.randint(own_keys[3], (OWN, PANELS), 0, NCP), jax.random.fold_in(own_keys[3], 1), 0, NCP - 1).astype(jnp.int32)
    owner_weight = jnp.clip(0.1 + 0.9 * jax.random.uniform(own_keys[4], (OWN, PANELS), jnp.float32) ** steps_of(own_keys[4], (OWN, PANELS), ((1, 16),), -0.2, 0.2), 0.1, 1.0)
    return dict(geometry=geometry, adjoint=adjoint, forward=forward, owner_map=owner_map, owner_weight=owner_weight)


FOUR_PI = 4.0 * math.pi
WAVENUM = 2.0 * math.pi * 6000.0 / 1500.0

def coupled_sum(target_geo, source_geo, panel_area, real_part, imag_part):
    offset = target_geo[0:3, :, None] - source_geo[0:3, None, :]
    radius = jnp.sqrt(lax.optimization_barrier(jnp.sum(offset * offset, axis=0)) + panel_area[None, :])
    inverse = 1.0 / radius
    phases = WAVENUM * radius
    green_re = jnp.cos(phases) * inverse / FOUR_PI
    green_im = jnp.sin(phases) * inverse / FOUR_PI
    slope_re = -WAVENUM * green_im - green_re * inverse
    slope_im = WAVENUM * green_re - green_im * inverse
    src_proj = -lax.optimization_barrier(jnp.sum(offset * source_geo[3:6, None, :], axis=0)) * inverse
    tgt_proj = lax.optimization_barrier(jnp.sum(offset * target_geo[3:6, :, None], axis=0)) * inverse
    kern_re = panel_area[None, :] * (slope_re * src_proj - slope_im * tgt_proj / WAVENUM)
    kern_im = panel_area[None, :] * (slope_im * src_proj + slope_re * tgt_proj / WAVENUM)
    return jnp.sum(kern_re * real_part - kern_im * imag_part)

def source_table(forward):
    half_rows = forward.shape[0] // 2
    rotated = jnp.concatenate([forward[half_rows:], -forward[:half_rows]], axis=0)
    return jnp.concatenate([forward, rotated], axis=1)

def tile_grads(target_geo, target_adj, source_geo, src_table):
    width = source_geo.shape[1]
    products = lax.dot_general(target_adj, src_table, (((0,), (0,)), ((), ())), precision=lax.Precision.HIGHEST, preferred_element_type=jnp.float32)
    grad_fn = jax.grad(coupled_sum, argnums=(0, 1))
    return grad_fn(target_geo[0:6], source_geo[0:6], source_geo[6], products[:, :width], products[:, width:])

def owner_add(totals, owners, weights, panel_grad):
    weighted = weights[:, None, :] * panel_grad[None, :, :]
    flat = jnp.transpose(weighted, (1, 0, 2)).reshape(6, -1)
    return totals.at[:, owners.reshape(-1)].add(flat)

def reference(geometry, adjoint, forward, owner_map, owner_weight):
    geo_groups = jnp.transpose(geometry.reshape(7, N_ROW, GROUP), (1, 0, 2))
    adj_groups = jnp.transpose(adjoint.reshape(2 * NDIR, N_ROW, GROUP), (1, 0, 2))
    fwd_groups = jnp.transpose(forward.reshape(2 * NDIR, N_ROW, GROUP), (1, 0, 2))

    def one_group(group_item):
        group_geo, group_adj, group_fwd = group_item
        src_table = source_table(group_fwd)

        def advance(src_total, block_index):
            first_index = (block_index * PAN_DEV).astype(jnp.int32)
            target_geo = lax.dynamic_slice_in_dim(group_geo, first_index, PAN_DEV, 1)
            target_adj = lax.dynamic_slice_in_dim(group_adj, first_index, PAN_DEV, 1)
            tgt_grad, src_grad = tile_grads(target_geo, target_adj, group_geo, src_table)
            return (src_total + src_grad, tgt_grad)
        src_total, tgt_blocks = lax.scan(advance, jnp.zeros((6, GROUP), jnp.float32), jnp.arange(N_LOOP, dtype=jnp.int32))
        return src_total + jnp.transpose(tgt_blocks, (1, 0, 2)).reshape(6, GROUP)
    grouped = lax.map(one_group, (geo_groups, adj_groups, fwd_groups))
    panel_grad = jnp.transpose(grouped, (1, 0, 2)).reshape(6, PANELS)
    return owner_add(jnp.zeros((6, NCP), jnp.float32), owner_map, owner_weight, panel_grad)
```

```python
import functools
import math

import jax
import jax.numpy as jnp
from jax import lax
from jax.experimental import pallas as pl
from jax.experimental.pallas import tpu as pltpu
from jax.sharding import PartitionSpec as P

WAVENUM = 2.0 * math.pi * 6000.0 / 1500.0
TURNS = WAVENUM / (2.0 * math.pi)
PAIR_SCALE = WAVENUM**3 / (4.0 * math.pi * TURNS)
F32 = jnp.float32
BF16 = jnp.bfloat16
TI = 256
TJ = 256
SUB = 16
LANE = 128

SIN_C = None
COS_C = None


def _fit(fn, odd, terms):
    import numpy as np

    nodes = 0.5 * np.cos(np.pi * (np.arange(400) + 0.5) / 400)
    cols = np.stack([nodes ** (2 * n + odd) for n in range(terms)], axis=1)
    coef = np.linalg.lstsq(cols, fn(nodes), rcond=None)[0]
    return [float(np.float32(c)) for c in coef]


def _tables():
    import numpy as np

    s = _fit(lambda t: math.sqrt(2.0) * np.sin(np.pi * t), 1, 5)
    c = _fit(lambda t: math.sqrt(2.0) * np.cos(np.pi * t), 0, 5)
    return s, c


SIN_C, COS_C = _tables()


def horner(coef, y):
    acc = coef[-1] * y + coef[-2]
    for c in coef[-3::-1]:
        acc = acc * y + c
    return acc


def hi_part(x):
    return x.astype(BF16).astype(F32)


def split3(x):
    one = hi_part(x)
    rest = x - one
    two = hi_part(rest)
    return one, two, rest - two


SPLIT_PAIRS = ((0, 0), (0, 1), (1, 0), (0, 2), (2, 0), (1, 1), (1, 2), (2, 1))


def rows8(x, n, a, b):
    return jnp.concatenate([x, n, a, b], axis=0)


def target_rows(geo, center):
    x = (geo[0:3] - center) * TURNS
    m = geo[3:6] * (1.0 / WAVENUM)
    ones = jnp.ones_like(x[0:1])
    xm = jnp.sum(x * m, axis=0, keepdims=True)
    return x, m, split3(rows8(x, m, ones, xm))


def target_table(adj, rows):
    hi = hi_part(adj)
    lo = adj - hi
    return jnp.concatenate([hi, hi, lo] + [rows[a] for a, _ in SPLIT_PAIRS], axis=0)


def source_rows(geo, center):
    x = (geo[0:3] - center) * TURNS
    n = geo[3:6]
    return x, n


def source_table(geo, fwd, x, n):
    area = geo[6:7]
    scaled = fwd * (area * PAIR_SCALE)
    re, im = scaled[0:32], scaled[32:64]
    real = jnp.concatenate([re, im], axis=0)
    imag = jnp.concatenate([im, -re], axis=0)
    rh, ih = hi_part(real), hi_part(imag)
    zero3 = jnp.zeros_like(x)
    zero1 = jnp.zeros_like(x[0:1])
    ones = jnp.ones_like(zero1)
    xn = jnp.sum(x * n, axis=0, keepdims=True)
    prow = split3(rows8(-n, zero3, xn, zero1))
    qrow = split3(rows8(zero3, -x, zero1, ones))
    zeros_w = jnp.zeros((192, x.shape[1]), F32)
    tail = jnp.zeros((64, x.shape[1]), F32)
    cols = [
        jnp.concatenate([rh, real - rh, rh, tail], axis=0),
        jnp.concatenate([ih, imag - ih, ih, tail], axis=0),
        jnp.concatenate([zeros_w] + [prow[b] for _, b in SPLIT_PAIRS], axis=0),
        jnp.concatenate([zeros_w] + [qrow[b] for _, b in SPLIT_PAIRS], axis=0),
    ]
    return cols


def pair_chunk(prod, xi, xj, area):
    wr, wi, pn, q = prod
    d0, d1, d2 = xi[0] - xj[0], xi[1] - xj[1], xi[2] - xj[2]
    r2 = (d0 * d0 + d1 * d1) + (d2 * d2 + area)
    rs = lax.rsqrt(r2)
    turns = r2 * rs
    t = turns - jnp.round(turns)
    v = rs * (1.0 / (2.0 * math.pi))
    y = t * t
    sv = (t * v) * horner(SIN_C, y)
    cv = v * horner(COS_C, y)
    es = sv * cv
    ec = v * v - sv * sv
    yr = ec * wr - es * wi
    yi = ec * wi + es * wr
    a = yi + v * yr
    b = yr - v * yi
    c = rs * ((q * yi - pn * yr) + (3.0 * v) * (pn * a + q * b))
    return a, b, c


def dot(a, b, dims=(((1,), (0,)), ((), ()))):
    return lax.dot_general(a, b, dims, preferred_element_type=F32)


def sum_splits(x):
    return x[0:8] + x[8:16] + x[16:24]


def pair_kernel(
    geo_a, geo_b, adj_a, adj_b, sgeo_a, sgeo_b, fwd_a, fwd_b, own_o, own_x, own_c, wt_o, wt_x, wt_c,
    out_ref,
    left, right, xi_ref, xj_ref, prod, abc, frow, fcol, tsum, ssum,
):
    width = geo_a.shape[1]
    total = 2 * width
    center = jnp.round(jnp.mean(geo_a[0:3], axis=1, keepdims=True))
    for part, (geo, adj) in enumerate(((geo_a, adj_a), (geo_b, adj_b))):
        cols = pl.ds(part * width, width)
        x, m, rows = target_rows(geo[...], center)
        left[cols, :] = target_table(adj[...], rows).T.astype(BF16)
        frow[:, cols] = jnp.concatenate(list(rows) + [jnp.zeros_like(rows[0])], axis=0).astype(BF16)
        xt = jnp.concatenate([x, m, m[0:2]], axis=0).T
        for k in range(3):
            xi_ref[k, cols, :] = jnp.broadcast_to(xt[:, k : k + 1], (width, LANE))
    for part, (geo, fwd) in enumerate(((sgeo_a, fwd_a), (sgeo_b, fwd_b))):
        cols = pl.ds(part * width, width)
        x, n = source_rows(geo[...], center)
        xj_ref[:, cols] = jnp.concatenate([x, geo[6:7] * (TURNS * TURNS)] * 2, axis=0)
        tab = source_table(geo[...], fwd[...], x, n)
        for k in range(4):
            right[k, :, cols] = tab[k].astype(BF16)
        ones = jnp.ones_like(x[0:1])
        rows = split3(rows8(x, n, ones, ones))
        frows = jnp.concatenate(list(rows) + [jnp.zeros_like(rows[0])], axis=0).astype(BF16)
        fcol[:, cols] = frows
    tsum[...] = jnp.zeros_like(tsum)
    ssum[...] = jnp.zeros_like(ssum)

    n_i, n_j = total // TI, total // TJ

    def tile(step, _):
        i0 = pl.multiple_of((step // n_j) * TI, TI)
        j0 = pl.multiple_of(lax.rem(step, n_j) * TJ, TJ)
        lhs = left[pl.ds(i0, TI), :]
        for k in range(4):
            prod[k] = dot(lhs, right[k, :, pl.ds(j0, TJ)])
        for jj in range(TJ // LANE):
            lanes = pl.ds(j0 + jj * LANE, LANE)
            xj = [xj_ref[k : k + 1, lanes] for k in range(4)]
            for ii in range(TI // SUB):
                rows = pl.ds(ii * SUB, SUB)
                xi = [xi_ref[k, pl.ds(i0 + ii * SUB, SUB), :] for k in range(3)]
                pr = [prod[k, rows, jj * LANE : (jj + 1) * LANE] for k in range(4)]
                for k, val in enumerate(pair_chunk(pr, xi, xj[0:3], xj[3])):
                    hi = val.astype(BF16)
                    abc[2 * k, rows, jj * LANE : (jj + 1) * LANE] = hi
                    abc[2 * k + 1, rows, jj * LANE : (jj + 1) * LANE] = (val - hi.astype(F32)).astype(BF16)
        fi = frow[:, pl.ds(i0, TI)]
        fj = fcol[:, pl.ds(j0, TJ)]
        for k in range(3):
            ssum[k, :, pl.ds(j0, TJ)] += dot(fi, abc[2 * k]) + dot(fi, abc[2 * k + 1])
            nt = (((1,), (1,)), ((), ()))
            tsum[k, :, pl.ds(i0, TI)] += dot(fj, abc[2 * k], nt) + dot(fj, abc[2 * k + 1], nt)
        return 0

    lax.fori_loop(0, n_i * n_j, tile, 0)

    tgt, src = [], []
    for part, (geo, sgeo) in enumerate(((geo_a, sgeo_a), (geo_b, sgeo_b))):
        cols = pl.ds(part * width, width)
        x = (geo[0:3] - center) * TURNS
        m = geo[3:6] * (1.0 / WAVENUM)
        sa, sb, sc = [sum_splits(tsum[k, :, cols]) for k in range(3)]
        gx = (2.0 * math.pi) * (x * sc[6:7] - sc[0:3]) + sa[3:6] - m * sb[6:7]
        gn = sb[0:3] - x * sb[6:7]
        tgt.append((gx * TURNS, gn * (1.0 / WAVENUM)))
        x = (sgeo[0:3] - center) * TURNS
        n = sgeo[3:6]
        sa, sb, sc = [sum_splits(ssum[k, :, cols]) for k in range(3)]
        gx = (2.0 * math.pi) * (x * sc[6:7] - sc[0:3]) - n * sa[6:7] + sb[3:6]
        gn = sa[0:3] - x * sa[6:7]
        src.append((gx * TURNS, gn))
    zero2 = jnp.zeros((2, width), F32)
    grads = [
        jnp.concatenate([tgt[0][0] + src[0][0], tgt[0][1] + src[0][1], zero2], axis=0),
        jnp.concatenate([tgt[1][0], tgt[1][1], zero2], axis=0),
        jnp.concatenate([src[1][0], src[1][1], zero2], axis=0),
    ]
    lhs = []
    for g in grads:
        hi = hi_part(g)
        lhs.append(jnp.concatenate([hi, g - hi], axis=0).astype(BF16))
    q_tile = 256
    owners = ((own_o, wt_o), (own_x, wt_x), (own_c, wt_c))

    def add_owner(step, _):
        q0 = pl.multiple_of(step * q_tile, q_tile)
        qs = q0 + lax.broadcasted_iota(jnp.int32, (q_tile, width), 0)
        acc = jnp.zeros((16, q_tile), F32)
        for g, (own, wt) in zip(lhs, owners):
            sel = jnp.zeros((q_tile, width), F32)
            for s in range(own.shape[0]):
                sel = sel + jnp.where(own[s : s + 1, :] == qs, wt[s : s + 1, :], 0.0)
            hi = sel.astype(BF16)
            lo = (sel - hi.astype(F32)).astype(BF16)
            nt = (((1,), (1,)), ((), ()))
            acc = acc + dot(g, hi, nt) + dot(g, lo, nt)
        out_ref[:, pl.ds(q0, q_tile)] = acc[0:8] + acc[8:16]
        return 0

    lax.fori_loop(0, out_ref.shape[1] // q_tile, add_owner, 0)


def pair_call(args, cp_total):
    width = args[0].shape[1]
    total = 2 * width
    return pl.pallas_call(
        pair_kernel,
        out_shape=jax.ShapeDtypeStruct((8, cp_total), F32),
        scratch_shapes=[
            pltpu.VMEM((total, 256), BF16),
            pltpu.VMEM((4, 256, total), BF16),
            pltpu.VMEM((3, total, LANE), F32),
            pltpu.VMEM((8, total), F32),
            pltpu.VMEM((4, TI, TJ), F32),
            pltpu.VMEM((6, TI, TJ), BF16),
            pltpu.VMEM((32, total), BF16),
            pltpu.VMEM((32, total), BF16),
            pltpu.VMEM((3, 32, total), F32),
            pltpu.VMEM((3, 32, total), F32),
        ],
        compiler_params=pltpu.CompilerParams(vmem_limit_bytes=48 * 1024 * 1024),
    )(*args)


def swap(x, axis, bit):
    size = lax.axis_size(axis)
    return lax.ppermute(x, axis, [(k, k ^ bit) for k in range(size)])


def halving(part, axes):
    cp_dev = part.shape[1]
    bits = []
    for axis in axes:
        size = lax.axis_size(axis)
        cp_dev //= size
        bits.append(size.bit_length() - 1)
    n_row, n_loop = bits
    cur = part[0:6].reshape([6] + [2] * (n_row + n_loop) + [cp_dev])
    order = list(range(n_row + n_loop, n_row, -1)) + list(range(n_row, 0, -1))
    cur = cur.transpose(order + [0, n_row + n_loop + 1]).reshape(-1, 6, cp_dev)
    steps = [("loop", 1 << b) for b in range(n_loop)] + [("row", 1 << b) for b in range(n_row)]
    for axis, bit in steps:
        half = cur.shape[0] // 2
        up = jnp.where((lax.axis_index(axis) & bit) > 0, 1, 0)
        keep = lax.dynamic_slice_in_dim(cur, up * half, half, 0)
        send = lax.dynamic_slice_in_dim(cur, (1 - up) * half, half, 0)
        cur = keep + swap(send, axis, bit)
    return cur[0]


def on_device(cp_dev, geometry, adjoint, forward, owner_map, owner_weight):
    cp_total = cp_dev * lax.axis_size("row") * lax.axis_size("loop")
    far = [swap(v, "loop", 2) for v in (adjoint, geometry, owner_map, owner_weight)]
    near = [swap(v, "loop", 1) for v in (forward, geometry, owner_map, owner_weight)]
    part = pair_call(
        (geometry, far[1], adjoint, far[0], geometry, near[1], forward, near[0],
         owner_map, far[2], near[2], owner_weight, far[3], near[3]),
        cp_total,
    )
    return halving(part, ("row", "loop"))


def solution(mesh):
    spec = P(None, ("parts", "row", "loop"))
    return jax.shard_map(
        functools.partial(on_device, 32), mesh=mesh, in_specs=(spec,) * 5, out_specs=spec, check_vma=False
    )
```

```python
import functools
import math

import jax
import jax.numpy as jnp
from jax import lax
from jax.experimental import pallas as pl
from jax.experimental.pallas import tpu as pltpu
from jax.sharding import PartitionSpec as P

WAVENUM = 2.0 * math.pi * 6000.0 / 1500.0
TURNS = WAVENUM / (2.0 * math.pi)
PAIR_SCALE = WAVENUM**3 / (4.0 * math.pi * TURNS)
F32 = jnp.float32
BF16 = jnp.bfloat16
TI = 256
TJ = 256
SUB = 16
LANE = 128

SIN_C = None
COS_C = None


def _fit(fn, odd, terms):
    import numpy as np

    nodes = 0.5 * np.cos(np.pi * (np.arange(400) + 0.5) / 400)
    cols = np.stack([nodes ** (2 * n + odd) for n in range(terms)], axis=1)
    coef = np.linalg.lstsq(cols, fn(nodes), rcond=None)[0]
    return [float(np.float32(c)) for c in coef]


def _tables():
    import numpy as np

    s = _fit(lambda t: math.sqrt(2.0) * np.sin(np.pi * t), 1, 5)
    c = _fit(lambda t: math.sqrt(2.0) * np.cos(np.pi * t), 0, 5)
    return s, c


SIN_C, COS_C = _tables()


def horner(coef, y):
    acc = coef[-1] * y + coef[-2]
    for c in coef[-3::-1]:
        acc = acc * y + c
    return acc


def hi_part(x):
    return x.astype(BF16).astype(F32)


def split3(x):
    one = hi_part(x)
    rest = x - one
    two = hi_part(rest)
    return one, two, rest - two


SPLIT_PAIRS = ((0, 0), (0, 1), (1, 0), (0, 2), (2, 0), (1, 1), (1, 2), (2, 1))


def rows8(x, n, a, b):
    return jnp.concatenate([x, n, a, b], axis=0)


def target_rows(geo, center):
    x = (geo[0:3] - center) * TURNS
    m = geo[3:6] * (1.0 / WAVENUM)
    ones = jnp.ones_like(x[0:1])
    xm = jnp.sum(x * m, axis=0, keepdims=True)
    return x, m, split3(rows8(x, m, ones, xm))


def target_table(adj, rows):
    hi = hi_part(adj)
    lo = adj - hi
    return jnp.concatenate([hi, hi, lo] + [rows[a] for a, _ in SPLIT_PAIRS], axis=0)


def source_rows(geo, center):
    x = (geo[0:3] - center) * TURNS
    n = geo[3:6]
    return x, n


def source_table(geo, fwd, x, n):
    area = geo[6:7]
    scaled = fwd * (area * PAIR_SCALE)
    re, im = scaled[0:32], scaled[32:64]
    real = jnp.concatenate([re, im], axis=0)
    imag = jnp.concatenate([im, -re], axis=0)
    rh, ih = hi_part(real), hi_part(imag)
    zero3 = jnp.zeros_like(x)
    zero1 = jnp.zeros_like(x[0:1])
    ones = jnp.ones_like(zero1)
    xn = jnp.sum(x * n, axis=0, keepdims=True)
    prow = split3(rows8(-n, zero3, xn, zero1))
    qrow = split3(rows8(zero3, -x, zero1, ones))
    zeros_w = jnp.zeros((192, x.shape[1]), F32)
    tail = jnp.zeros((64, x.shape[1]), F32)
    cols = [
        jnp.concatenate([rh, real - rh, rh, tail], axis=0),
        jnp.concatenate([ih, imag - ih, ih, tail], axis=0),
        jnp.concatenate([zeros_w] + [prow[b] for _, b in SPLIT_PAIRS], axis=0),
        jnp.concatenate([zeros_w] + [qrow[b] for _, b in SPLIT_PAIRS], axis=0),
    ]
    return cols


def pair_chunk(prod, xi, xj, area):
    wr, wi, pn, q = prod
    d0, d1, d2 = xi[0] - xj[0], xi[1] - xj[1], xi[2] - xj[2]
    r2 = (d0 * d0 + d1 * d1) + (d2 * d2 + area)
    rs = lax.rsqrt(r2)
    turns = r2 * rs
    t = turns - jnp.round(turns)
    v = rs * (1.0 / (2.0 * math.pi))
    y = t * t
    sv = (t * v) * horner(SIN_C, y)
    cv = v * horner(COS_C, y)
    es = sv * cv
    ec = v * v - sv * sv
    yr = ec * wr - es * wi
    yi = ec * wi + es * wr
    a = yi + v * yr
    b = yr - v * yi
    c = rs * ((q * yi - pn * yr) + (3.0 * v) * (pn * a + q * b))
    return a, b, c


def dot(a, b, dims=(((1,), (0,)), ((), ()))):
    return lax.dot_general(a, b, dims, preferred_element_type=F32)


def sum_splits(x):
    return x[0:8] + x[8:16] + x[16:24]


NT = (((1,), (1,)), ((), ()))


def build_targets(geo, adj, center, cols, left, xi_ref, frow):
    x, m, rows = target_rows(geo, center)
    left[cols, :] = target_table(adj, rows).T.astype(BF16)
    frow[:, cols] = jnp.concatenate(list(rows) + [jnp.zeros_like(rows[0])], axis=0).astype(BF16)
    xt = jnp.concatenate([x, m, m[0:2]], axis=0).T
    for k in range(3):
        xi_ref[k, cols, :] = jnp.broadcast_to(xt[:, k : k + 1], (x.shape[1], LANE))


def build_sources(geo, fwd, center, cols, right, xj_ref, fcol):
    x, n = source_rows(geo, center)
    xj_ref[:, cols] = jnp.concatenate([x, geo[6:7] * (TURNS * TURNS)] * 2, axis=0)
    tab = source_table(geo, fwd, x, n)
    for k in range(4):
        right[k, :, cols] = tab[k].astype(BF16)
    ones = jnp.ones_like(x[0:1])
    rows = split3(rows8(x, n, ones, ones))
    fcol[:, cols] = jnp.concatenate(list(rows) + [jnp.zeros_like(rows[0])], axis=0).astype(BF16)


def center_of(geo):
    return jnp.round(jnp.mean(geo[0:3], axis=1, keepdims=True))


def run_tiles(count, place, left, right, xi_ref, xj_ref, frow, fcol, prod, abc, tsum, ssum):
    def start(t):
        i0, j0 = place(t)
        return pl.multiple_of(i0, TI), pl.multiple_of(j0, TJ)

    def products(t, slot):
        i0, j0 = start(t)
        lhs = left[pl.ds(i0, TI), :]
        for k in range(4):
            prod[slot, k] = dot(lhs, right[k, :, pl.ds(j0, TJ)])

    def values(t, slot):
        i0, j0 = start(t)
        for jj in range(TJ // LANE):
            lanes = pl.ds(j0 + jj * LANE, LANE)
            here = slice(jj * LANE, (jj + 1) * LANE)
            xj = [xj_ref[k : k + 1, lanes] for k in range(4)]
            for ii in range(TI // SUB):
                rows = pl.ds(ii * SUB, SUB)
                xi = [xi_ref[k, pl.ds(i0 + ii * SUB, SUB), :] for k in range(3)]
                pr = [prod[slot, k, rows, here] for k in range(4)]
                for k, val in enumerate(pair_chunk(pr, xi, xj[0:3], xj[3])):
                    hi = val.astype(BF16)
                    abc[slot, 2 * k, rows, here] = hi
                    abc[slot, 2 * k + 1, rows, here] = (val - hi.astype(F32)).astype(BF16)

    def sums(t, slot):
        i0, j0 = start(t)
        fi = frow[:, pl.ds(i0, TI)]
        fj = fcol[:, pl.ds(j0, TJ)]
        for k in range(3):
            ssum[k, :, pl.ds(j0, TJ)] += dot(fi, abc[slot, 2 * k]) + dot(fi, abc[slot, 2 * k + 1])
            tsum[k, :, pl.ds(i0, TI)] += dot(fj, abc[slot, 2 * k], NT) + dot(fj, abc[slot, 2 * k + 1], NT)

    last = count - 1
    products(0, 0)
    abc[1] = jnp.zeros_like(abc[1])

    def double(u, _):
        t = 2 * u
        products(t + 1, 1)
        values(t, 0)
        sums(jnp.maximum(t - 1, 0), 1)
        products(jnp.minimum(t + 2, last), 0)
        values(t + 1, 1)
        sums(t, 0)
        return 0

    lax.fori_loop(0, count // 2, double, 0)
    sums(last, 1)


def own_kernel(geo, adj, fwd, left, right, xi_ref, tsum, ssum, xj_ref, frow, fcol, prod, abc):
    width = geo.shape[1]
    center = center_of(geo)
    cols = pl.ds(0, width)
    build_targets(geo[...], adj[...], center, cols, left, xi_ref, frow)
    build_sources(geo[...], fwd[...], center, cols, right, xj_ref, fcol)
    tsum[...] = jnp.zeros_like(tsum)
    ssum[...] = jnp.zeros_like(ssum)
    n_j = width // TJ
    run_tiles(
        (width // TI) * n_j, lambda t: ((t // n_j) * TI, lax.rem(t, n_j) * TJ),
        left, right, xi_ref, xj_ref, frow, fcol, prod, abc, tsum, ssum,
    )


def sum_splits(x):
    return x[0:8] + x[8:16] + x[16:24]


def rest_kernel(
    geo, far, near, own, wt, left_o, right_o, xi_o, tsum_o, ssum_o,
    out_ref,
    left, right, xi_ref, xj_ref, frow, fcol, prod, abc, tsum, ssum,
):
    width = geo.shape[1]
    center = center_of(geo)
    first, second = pl.ds(0, width), pl.ds(width, width)
    left[first, :] = left_o[...]
    right[:, :, first] = right_o[...]
    xi_ref[:, first, :] = xi_o[...]
    x, m, rows = target_rows(geo[...], center)
    frow[:, first] = jnp.concatenate(list(rows) + [jnp.zeros_like(rows[0])], axis=0).astype(BF16)
    ones = jnp.ones_like(x[0:1])
    rows = split3(rows8(x, geo[3:6], ones, ones))
    fcol[:, first] = jnp.concatenate(list(rows) + [jnp.zeros_like(rows[0])], axis=0).astype(BF16)
    xj_ref[:, first] = jnp.concatenate([x, geo[6:7] * (TURNS * TURNS)] * 2, axis=0)
    tsum[:, :, first] = tsum_o[...]
    ssum[:, :, first] = ssum_o[...]
    tsum[:, :, second] = jnp.zeros_like(tsum_o)
    ssum[:, :, second] = jnp.zeros_like(ssum_o)
    build_targets(far[64:71], far[0:64], center, second, left, xi_ref, frow)
    build_sources(near[64:71], near[0:64], center, second, right, xj_ref, fcol)

    n_i, n_j = width // TI, width // TJ
    block = n_i * n_j

    def place(t):
        b = t // block
        inner = lax.rem(t, block)
        i0 = jnp.where(b > 0, width, 0) + (inner // n_j) * TI
        j0 = jnp.where(b == 1, 0, width) + lax.rem(inner, n_j) * TJ
        return i0, j0

    run_tiles(3 * block, place, left, right, xi_ref, xj_ref, frow, fcol, prod, abc, tsum, ssum)

    def target_grad(g, cols):
        x = (g[0:3] - center) * TURNS
        m = g[3:6] * (1.0 / WAVENUM)
        sa, sb, sc = [sum_splits(tsum[k, :, cols]) for k in range(3)]
        gx = (2.0 * math.pi) * (x * sc[6:7] - sc[0:3]) + sa[3:6] - m * sb[6:7]
        gn = sb[0:3] - x * sb[6:7]
        return gx * TURNS, gn * (1.0 / WAVENUM)

    def source_grad(g, cols):
        x = (g[0:3] - center) * TURNS
        n = g[3:6]
        sa, sb, sc = [sum_splits(ssum[k, :, cols]) for k in range(3)]
        gx = (2.0 * math.pi) * (x * sc[6:7] - sc[0:3]) - n * sa[6:7] + sb[3:6]
        gn = sa[0:3] - x * sa[6:7]
        return gx * TURNS, gn

    t_own, s_own = target_grad(geo, first), source_grad(geo, first)
    zero2 = jnp.zeros((2, width), F32)
    grads = [
        (t_own[0] + s_own[0], t_own[1] + s_own[1]),
        target_grad(far[64:71], second),
        source_grad(near[64:71], second),
    ]
    lhs = []
    for gx, gn in grads:
        g = jnp.concatenate([gx, gn, zero2], axis=0)
        hi = hi_part(g)
        lhs.append(jnp.concatenate([hi, g - hi], axis=0).astype(BF16))
    q_tile = 256
    owners = (
        (own[...].astype(F32), wt[...]), (far[76:80], far[72:76]), (near[76:80], near[72:76])
    )

    def add_owner(step, _):
        q0 = pl.multiple_of(step * q_tile, q_tile)
        qs = (q0 + lax.broadcasted_iota(jnp.int32, (q_tile, width), 0)).astype(F32)
        acc = jnp.zeros((16, q_tile), F32)
        for g, (who, weight) in zip(lhs, owners):
            sel = jnp.zeros((q_tile, width), F32)
            for s in range(4):
                sel = sel + jnp.where(who[s : s + 1, :] == qs, weight[s : s + 1, :], 0.0)
            hi = sel.astype(BF16)
            lo = (sel - hi.astype(F32)).astype(BF16)
            acc = acc + dot(g, hi, NT) + dot(g, lo, NT)
        out_ref[:, pl.ds(q0, q_tile)] = acc[0:8] + acc[8:16]
        return 0

    lax.fori_loop(0, out_ref.shape[1] // q_tile, add_owner, 0)


def shape(dims, kind):
    return jax.ShapeDtypeStruct(dims, kind)


def tile_scratch():
    return [pltpu.VMEM((2, 4, TI, TJ), F32), pltpu.VMEM((2, 6, TI, TJ), BF16)]


PARAMS = pltpu.CompilerParams(vmem_limit_bytes=40 * 1024 * 1024)


def own_call(geo, adj, fwd):
    width = geo.shape[1]
    return pl.pallas_call(
        own_kernel,
        out_shape=[
            shape((width, 256), BF16), shape((4, 256, width), BF16), shape((3, width, LANE), F32),
            shape((3, 32, width), F32), shape((3, 32, width), F32),
        ],
        scratch_shapes=[pltpu.VMEM((8, width), F32), pltpu.VMEM((32, width), BF16), pltpu.VMEM((32, width), BF16)]
        + tile_scratch(),
        compiler_params=PARAMS,
        cost_estimate=pl.CostEstimate(flops=4 * 10**9, bytes_accessed=4 * 10**6, transcendentals=0),
        name="own",
    )(geo, adj, fwd)


def rest_call(args, cp_total):
    width = args[0].shape[1]
    total = 2 * width
    return pl.pallas_call(
        rest_kernel,
        out_shape=shape((8, cp_total), F32),
        scratch_shapes=[
            pltpu.VMEM((total, 256), BF16),
            pltpu.VMEM((4, 256, total), BF16),
            pltpu.VMEM((3, total, LANE), F32),
            pltpu.VMEM((8, total), F32),
            pltpu.VMEM((32, total), BF16),
            pltpu.VMEM((32, total), BF16),
        ]
        + tile_scratch()
        + [pltpu.VMEM((3, 32, total), F32), pltpu.VMEM((3, 32, total), F32)],
        compiler_params=PARAMS,
        cost_estimate=pl.CostEstimate(flops=12 * 10**9, bytes_accessed=4 * 10**6, transcendentals=0),
        name="rest",
    )(*args)


def swap(x, axis, bit):
    size = lax.axis_size(axis)
    return lax.ppermute(x, axis, [(k, k ^ bit) for k in range(size)])


def halving(part, axes):
    cp_dev = part.shape[1]
    bits = []
    for axis in axes:
        size = lax.axis_size(axis)
        cp_dev //= size
        bits.append(size.bit_length() - 1)
    n_row, n_loop = bits
    cur = part[0:6].reshape([6] + [2] * (n_row + n_loop) + [cp_dev])
    order = list(range(n_row + n_loop, n_row, -1)) + list(range(n_row, 0, -1))
    cur = cur.transpose(order + [0, n_row + n_loop + 1]).reshape(-1, 6, cp_dev)
    steps = [("loop", 1 << b) for b in range(n_loop)] + [("row", 1 << b) for b in range(n_row)]
    for axis, bit in steps:
        half = cur.shape[0] // 2
        up = jnp.where((lax.axis_index(axis) & bit) > 0, 1, 0)
        keep = lax.dynamic_slice_in_dim(cur, up * half, half, 0)
        send = lax.dynamic_slice_in_dim(cur, (1 - up) * half, half, 0)
        cur = keep + swap(send, axis, bit)
    return cur[0]


def on_device(cp_dev, geometry, adjoint, forward, owner_map, owner_weight):
    cp_total = cp_dev * lax.axis_size("row") * lax.axis_size("loop")
    tail = [geometry, jnp.zeros_like(owner_weight[0:1]), owner_weight, owner_map.astype(F32)]
    far = swap(jnp.concatenate([adjoint] + tail, axis=0), "loop", 2)
    near = swap(jnp.concatenate([forward] + tail, axis=0), "loop", 1)
    tables = own_call(geometry, adjoint, forward)
    part = rest_call((geometry, far, near, owner_map, owner_weight, *tables), cp_total)
    return halving(part, ("row", "loop"))


def solution(mesh):
    spec = P(None, ("parts", "row", "loop"))
    return jax.shard_map(
        functools.partial(on_device, 32), mesh=mesh, in_specs=(spec,) * 5, out_specs=spec, check_vma=False
    )
```

```python
import functools
import math

import jax
import jax.numpy as jnp
from jax import lax
from jax.experimental import pallas as pl
from jax.experimental.pallas import tpu as pltpu
from jax.sharding import PartitionSpec as P

WAVENUM = 2.0 * math.pi * 6000.0 / 1500.0
TURNS = WAVENUM / (2.0 * math.pi)
PAIR_SCALE = WAVENUM**3 / (4.0 * math.pi * TURNS)
F32 = jnp.float32
BF16 = jnp.bfloat16
TI = 256
TJ = 256
SUB = 16
LANE = 128

SIN_C = None
COS_C = None


def _fit(fn, odd, terms):
    import numpy as np

    nodes = 0.5 * np.cos(np.pi * (np.arange(400) + 0.5) / 400)
    cols = np.stack([nodes ** (2 * n + odd) for n in range(terms)], axis=1)
    coef = np.linalg.lstsq(cols, fn(nodes), rcond=None)[0]
    return [float(np.float32(c)) for c in coef]


def _tables():
    import numpy as np

    s = _fit(lambda t: math.sqrt(2.0) * np.sin(np.pi * t), 1, 4)
    c = _fit(lambda t: math.sqrt(2.0) * np.cos(np.pi * t), 0, 5)
    return s, c


SIN_C, COS_C = _tables()


def horner(coef, y):
    acc = coef[-1] * y + coef[-2]
    for c in coef[-3::-1]:
        acc = acc * y + c
    return acc


def hi_part(x):
    return x.astype(BF16).astype(F32)


def split3(x):
    one = hi_part(x)
    rest = x - one
    two = hi_part(rest)
    return one, two, rest - two


SPLIT_PAIRS = ((0, 0), (0, 1), (1, 0), (0, 2), (2, 0), (1, 1), (1, 2), (2, 1))


def rows8(x, n, a, b):
    return jnp.concatenate([x, n, a, b], axis=0)


def target_rows(geo, center):
    x = (geo[0:3] - center) * TURNS
    m = geo[3:6] * (1.0 / WAVENUM)
    ones = jnp.ones_like(x[0:1])
    xm = jnp.sum(x * m, axis=0, keepdims=True)
    return x, m, split3(rows8(x, m, ones, xm))


def target_table(adj, rows):
    hi = hi_part(adj)
    lo = adj - hi
    return jnp.concatenate([hi, hi, lo] + [rows[a] for a, _ in SPLIT_PAIRS], axis=0)


def source_rows(geo, center):
    x = (geo[0:3] - center) * TURNS
    n = geo[3:6]
    return x, n


def source_table(geo, fwd, x, n):
    area = geo[6:7]
    scaled = fwd * (area * PAIR_SCALE)
    re, im = scaled[0:32], scaled[32:64]
    real = jnp.concatenate([re, im], axis=0)
    imag = jnp.concatenate([im, -re], axis=0)
    rh, ih = hi_part(real), hi_part(imag)
    zero3 = jnp.zeros_like(x)
    zero1 = jnp.zeros_like(x[0:1])
    ones = jnp.ones_like(zero1)
    xn = jnp.sum(x * n, axis=0, keepdims=True)
    prow = split3(rows8(-n, zero3, xn, zero1))
    qrow = split3(rows8(zero3, -x, zero1, ones))
    zeros_w = jnp.zeros((192, x.shape[1]), F32)
    tail = jnp.zeros((64, x.shape[1]), F32)
    cols = [
        jnp.concatenate([rh, real - rh, rh, tail], axis=0),
        jnp.concatenate([ih, imag - ih, ih, tail], axis=0),
        jnp.concatenate([zeros_w] + [prow[b] for _, b in SPLIT_PAIRS], axis=0),
        jnp.concatenate([zeros_w] + [qrow[b] for _, b in SPLIT_PAIRS], axis=0),
    ]
    return cols


def pair_chunk(prod, xi, xj, area):
    wr, wi, pn, q = prod
    d0, d1, d2 = xi[0] - xj[0], xi[1] - xj[1], xi[2] - xj[2]
    r2 = (d0 * d0 + d1 * d1) + (d2 * d2 + area)
    rs = lax.rsqrt(r2)
    turns = r2 * rs
    t = turns - jnp.round(turns)
    v = rs * (1.0 / (2.0 * math.pi))
    y = t * t
    sv = (t * v) * horner(SIN_C, y)
    cv = v * horner(COS_C, y)
    es = sv * cv
    ec = v * v - sv * sv
    yr = ec * wr - es * wi
    yi = ec * wi + es * wr
    a = yi + v * yr
    b = yr - v * yi
    c = rs * ((q * yi - pn * yr) + (3.0 * v) * (pn * a + q * b))
    return a, b, c


def dot(a, b, dims=(((1,), (0,)), ((), ()))):
    return lax.dot_general(a, b, dims, preferred_element_type=F32)


def sum_splits(x):
    return x[0:8] + x[8:16] + x[16:24]


NT = (((1,), (1,)), ((), ()))


def sum_rows(x, n):
    width = x.shape[1]
    zero = jnp.zeros((1, width), F32)
    x1, x2, x3 = split3(x)
    n1 = hi_part(n)
    xr = jnp.concatenate([x1, jnp.ones_like(zero), x2, zero, x3, zero], axis=0)
    nr = jnp.concatenate([n1, zero, n - n1, zero], axis=0)
    z12, z20 = jnp.zeros((12, width), F32), jnp.zeros((20, width), F32)
    rows = ([xr, z20], [z12, nr, z12], [z20, xr])
    return [jnp.concatenate(r, axis=0).astype(BF16) for r in rows]


def read_sums(acc):
    return acc[0:4] + acc[4:8] + acc[8:12], acc[12:15] + acc[16:19], acc[20:24] + acc[24:28] + acc[28:32]


def build_targets(geo, adj, center, cols, left, xi_ref, frow):
    x, m, rows = target_rows(geo, center)
    left[cols, :] = target_table(adj, rows).T.astype(BF16)
    sums = sum_rows(x, m)
    for k in range(3):
        frow[k, :, cols] = sums[k]
    xt = jnp.concatenate([x, m, m[0:2]], axis=0).T
    for k in range(3):
        xi_ref[k, cols, :] = jnp.broadcast_to(xt[:, k : k + 1], (x.shape[1], LANE))


def build_sources(geo, fwd, center, cols, right, xj_ref, fcol):
    x, n = source_rows(geo, center)
    xj_ref[:, cols] = jnp.concatenate([x, geo[6:7] * (TURNS * TURNS)] * 2, axis=0)
    tab = source_table(geo, fwd, x, n)
    for k in range(4):
        right[k, :, cols] = tab[k].astype(BF16)
    sums = sum_rows(x, n)
    for k, part in enumerate((sums[1], sums[0], sums[2])):
        fcol[k, :, cols] = part


def center_of(geo):
    return jnp.round(jnp.mean(geo[0:3], axis=1, keepdims=True))


def run_tiles(count, place, left, right, xi_ref, xj_ref, frow, fcol, prod, abc, tsum, ssum):
    def start(t):
        i0, j0 = place(t)
        return pl.multiple_of(i0, TI), pl.multiple_of(j0, TJ)

    def products(t, slot):
        i0, j0 = start(t)

        def piece(k):
            prod[slot, k] = dot(left[pl.ds(i0, TI), :], right[k, :, pl.ds(j0, TJ)])

        return [functools.partial(piece, k) for k in range(4)]

    def values(t, slot):
        i0, j0 = start(t)

        def piece(jj, ii):
            lanes = pl.ds(j0 + jj * LANE, LANE)
            here = slice(jj * LANE, (jj + 1) * LANE)
            xj = [xj_ref[k : k + 1, lanes] for k in range(4)]
            rows = pl.ds(ii * SUB, SUB)
            xi = [xi_ref[k, pl.ds(i0 + ii * SUB, SUB), :] for k in range(3)]
            pr = [prod[slot, k, rows, here] for k in range(4)]
            for k, val in enumerate(pair_chunk(pr, xi, xj[0:3], xj[3])):
                hi = val.astype(BF16)
                abc[slot, 2 * k, rows, here] = hi
                abc[slot, 2 * k + 1, rows, here] = (val - hi.astype(F32)).astype(BF16)

        return [functools.partial(piece, jj, ii) for jj in range(TJ // LANE) for ii in range(TI // SUB)]

    def sums(t, slot):
        i0, j0 = start(t)
        kept = [None, None]

        def piece(k):
            fi = frow[k, :, pl.ds(i0, TI)]
            hi, lo = abc[slot, 2 * k], abc[slot, 2 * k + 1]
            add = dot(jnp.concatenate([fi, fi], axis=1), jnp.concatenate([hi, lo], axis=0))
            kept[0] = add if k == 0 else kept[0] + add
            if k == 2:
                ssum[:, pl.ds(j0, TJ)] += kept[0]

        def other(k):
            fj = fcol[k, :, pl.ds(j0, TJ)]
            hi, lo = abc[slot, 2 * k], abc[slot, 2 * k + 1]
            add = dot(jnp.concatenate([fj, fj], axis=1), jnp.concatenate([hi, lo], axis=1), NT)
            kept[1] = add if k == 0 else kept[1] + add
            if k == 2:
                tsum[:, pl.ds(i0, TI)] += kept[1]

        return [functools.partial(f, k) for f in (piece, other) for k in range(3)]

    def interleave(vector, matrix):
        gap = len(vector) // len(matrix)
        for n, todo in enumerate(vector):
            if n % gap == 0 and n // gap < len(matrix):
                matrix[n // gap]()
            todo()

    last = count - 1
    for todo in products(0, 0):
        todo()
    abc[1] = jnp.zeros_like(abc[1])

    def double(u, _):
        t = 2 * u
        interleave(values(t, 0), products(t + 1, 1) + sums(jnp.maximum(t - 1, 0), 1))
        interleave(values(t + 1, 1), products(jnp.minimum(t + 2, last), 0) + sums(t, 0))
        return 0

    lax.fori_loop(0, count // 2, double, 0)
    for todo in sums(last, 1):
        todo()


def pack_kernel(geo, adj, fwd, own, wt, tpack, spack, geo_v, own_v, wt_v, sems):
    copies = [
        pltpu.make_async_copy(src, dst, sems.at[k])
        for k, (src, dst) in enumerate(
            ((adj, tpack.at[0:64]), (fwd, spack.at[0:64]), (geo, geo_v), (own, own_v), (wt, wt_v))
        )
    ]
    for c in copies:
        c.start()
    for c in copies[2:]:
        c.wait()
    geo_rows = jnp.concatenate([geo_v[...], jnp.zeros_like(geo_v[0:1])], axis=0)
    own_rows = jnp.concatenate([wt_v[...], own_v[...].astype(F32)], axis=0)
    for pack in (tpack, spack):
        pack[64:72] = geo_rows
        pack[72:80] = own_rows
    for c in copies[:2]:
        c.wait()


def own_kernel(geo_ref, adj, fwd, left, right, xi_ref, tsum, ssum, xj_ref, frow, fcol, prod, abc):
    width = geo_ref.shape[1]
    geo = geo_ref[...]
    center = center_of(geo)
    cols = pl.ds(0, width)
    build_targets(geo, adj[...], center, cols, left, xi_ref, frow)
    build_sources(geo, fwd[...], center, cols, right, xj_ref, fcol)
    tsum[...] = jnp.zeros_like(tsum)
    ssum[...] = jnp.zeros_like(ssum)
    n_j = width // TJ
    run_tiles(
        (width // TI) * n_j, lambda t: ((t // n_j) * TI, lax.rem(t, n_j) * TJ),
        left, right, xi_ref, xj_ref, frow, fcol, prod, abc, tsum, ssum,
    )


def reverse_bits(x, bits):
    out = jnp.zeros_like(x)
    for b in range(bits):
        out = out | (((x >> b) & 1) << (bits - 1 - b))
    return out


def rest_kernel(
    tpack, far, near, left_o, right_o, xi_o, tsum_o, ssum_o,
    out_ref,
    left, right, xi_ref, xj_ref, frow, fcol, prod, abc, tsum, ssum,
):
    width = tpack.shape[1]
    geo = tpack[64:71]
    center = center_of(geo)
    first, second = pl.ds(0, width), pl.ds(width, width)
    left[first, :] = left_o[...]
    right[:, :, first] = right_o[...]
    xi_ref[:, first, :] = xi_o[...]
    x, n = source_rows(geo, center)
    tsums, ssums = sum_rows(x, n * (1.0 / WAVENUM)), sum_rows(x, n)
    for k in range(3):
        frow[k, :, first] = tsums[k]
        fcol[k, :, first] = ssums[(1, 0, 2)[k]]
    xj_ref[:, first] = jnp.concatenate([x, geo[6:7] * (TURNS * TURNS)] * 2, axis=0)
    tsum[:, first] = tsum_o[...]
    ssum[:, first] = ssum_o[...]
    tsum[:, second] = jnp.zeros_like(tsum_o)
    ssum[:, second] = jnp.zeros_like(ssum_o)
    build_targets(far[64:71], far[0:64], center, second, left, xi_ref, frow)
    build_sources(near[64:71], near[0:64], center, second, right, xj_ref, fcol)

    n_i, n_j = width // TI, width // TJ
    block = n_i * n_j

    def place(t):
        b = t // block
        inner = lax.rem(t, block)
        i0 = jnp.where(b > 0, width, 0) + (inner // n_j) * TI
        j0 = jnp.where(b == 1, 0, width) + lax.rem(inner, n_j) * TJ
        return i0, j0

    run_tiles(3 * block, place, left, right, xi_ref, xj_ref, frow, fcol, prod, abc, tsum, ssum)

    def target_grad(g, cols):
        x = (g[0:3] - center) * TURNS
        m = g[3:6] * (1.0 / WAVENUM)
        sb, an, sc = read_sums(tsum[:, cols])
        gx = (2.0 * math.pi) * (x * sc[3:4] - sc[0:3]) + an - m * sb[3:4]
        gn = sb[0:3] - x * sb[3:4]
        return gx * TURNS, gn * (1.0 / WAVENUM)

    def source_grad(g, cols):
        x = (g[0:3] - center) * TURNS
        n = g[3:6]
        sa, bm, sc = read_sums(ssum[:, cols])
        gx = (2.0 * math.pi) * (x * sc[3:4] - sc[0:3]) - n * sa[3:4] + bm
        gn = sa[0:3] - x * sa[3:4]
        return gx * TURNS, gn

    t_own, s_own = target_grad(geo, first), source_grad(geo, first)
    zero2 = jnp.zeros((2, width), F32)
    grads = [
        (t_own[0] + s_own[0], t_own[1] + s_own[1]),
        target_grad(far[64:71], second),
        source_grad(near[64:71], second),
    ]
    slots, _, cp_dev = out_ref.shape
    low_iota = lax.broadcasted_iota(jnp.int32, (cp_dev, width), 0)
    terms = []
    for (gx, gn), pack in zip(grads, (tpack, far, near)):
        g = jnp.concatenate([gx, gn, zero2], axis=0)
        own, wt = pack[76:80].astype(jnp.int32), pack[72:76]
        place_of = reverse_bits(own // cp_dev, slots.bit_length() - 1)
        low = lax.rem(own, cp_dev)
        for s in range(4):
            gw = g * wt[s : s + 1]
            hi = hi_part(gw)
            here = jnp.where(low[s : s + 1] == low_iota, 1.0, 0.0).astype(BF16)
            terms.append((place_of[s : s + 1], hi, gw - hi, here))
    onehot = jnp.concatenate([t[3] for t in terms], axis=1)

    def add_owner(step, _):
        s0 = step * 16
        cols = []
        for where_to, hi, lo, _ in terms:
            rows = []
            for r in range(16):
                mask = where_to == s0 + r
                rows += [jnp.where(mask, hi, 0.0), jnp.where(mask, lo, 0.0)]
            cols.append(jnp.concatenate(rows, axis=0).astype(BF16))
        acc = dot(jnp.concatenate(cols, axis=1), onehot, NT).reshape(16, 16, cp_dev)
        out_ref[pl.ds(s0, 16)] = acc[:, 0:8] + acc[:, 8:16]
        return 0

    if slots == 16:
        add_owner(0, 0)
    else:
        lax.fori_loop(0, slots // 16, add_owner, 0)


def shape(dims, kind):
    return jax.ShapeDtypeStruct(dims, kind)


def tile_scratch():
    return [pltpu.VMEM((2, 4, TI, TJ), F32), pltpu.VMEM((2, 6, TI, TJ), BF16)]


PARAMS = pltpu.CompilerParams(vmem_limit_bytes=20 * 1024 * 1024)


def pack_call(geo, adj, fwd, own, wt):
    width = geo.shape[1]
    return pl.pallas_call(
        pack_kernel,
        in_specs=[pl.BlockSpec(memory_space=pl.ANY)] * 5,
        out_shape=[shape((80, width), F32)] * 2,
        scratch_shapes=[
            pltpu.VMEM((7, width), F32), pltpu.VMEM((4, width), jnp.int32), pltpu.VMEM((4, width), F32),
            pltpu.SemaphoreType.DMA((5,)),
        ],
        name="pack",
    )(geo, adj, fwd, own, wt)


def own_call(geo, adj, fwd):
    width = geo.shape[1]
    return pl.pallas_call(
        own_kernel,
        out_shape=[
            shape((width, 256), BF16), shape((4, 256, width), BF16), shape((3, width, LANE), F32),
            shape((32, width), F32), shape((32, width), F32),
        ],
        scratch_shapes=[
            pltpu.VMEM((8, width), F32), pltpu.VMEM((3, 32, width), BF16), pltpu.VMEM((3, 32, width), BF16)
        ]
        + tile_scratch(),
        compiler_params=PARAMS,
        cost_estimate=pl.CostEstimate(flops=4 * 10**9, bytes_accessed=4 * 10**6, transcendentals=0),
        name="own",
    )(geo, adj, fwd)


def rest_call(args, slots, cp_dev):
    width = args[0].shape[1]
    total = 2 * width
    return pl.pallas_call(
        rest_kernel,
        out_shape=shape((slots, 8, cp_dev), F32),
        scratch_shapes=[
            pltpu.VMEM((total, 256), BF16),
            pltpu.VMEM((4, 256, total), BF16),
            pltpu.VMEM((3, total, LANE), F32),
            pltpu.VMEM((8, total), F32),
            pltpu.VMEM((3, 32, total), BF16),
            pltpu.VMEM((3, 32, total), BF16),
        ]
        + tile_scratch()
        + [pltpu.VMEM((32, total), F32), pltpu.VMEM((32, total), F32)],
        compiler_params=PARAMS,
        cost_estimate=pl.CostEstimate(flops=12 * 10**9, bytes_accessed=4 * 10**6, transcendentals=0),
        name="rest",
    )(*args)


def swap(x, axis, bit):
    size = lax.axis_size(axis)
    return lax.ppermute(x, axis, [(k, k ^ bit) for k in range(size)])


def halving(cur):
    n_loop = lax.axis_size("loop").bit_length() - 1
    n_row = lax.axis_size("row").bit_length() - 1
    steps = [("loop", 1 << b) for b in range(n_loop)] + [("row", 1 << b) for b in range(n_row)]
    for axis, bit in steps:
        half = cur.shape[0] // 2
        up = jnp.where((lax.axis_index(axis) & bit) > 0, 1, 0)
        keep = lax.dynamic_slice_in_dim(cur, up * half, half, 0)
        send = lax.dynamic_slice_in_dim(cur, (1 - up) * half, half, 0)
        cur = keep + swap(send, axis, bit)
    return cur[0, 0:6]


def on_device(cp_dev, geometry, adjoint, forward, owner_map, owner_weight):
    slots = lax.axis_size("row") * lax.axis_size("loop")
    tpack, spack = pack_call(geometry, adjoint, forward, owner_map, owner_weight)
    far = swap(tpack, "loop", 2)
    near = swap(spack, "loop", 1)
    tables = own_call(geometry, adjoint, forward)
    return halving(rest_call((tpack, far, near, *tables), slots, cp_dev))


def solution(mesh):
    spec = P(None, ("parts", "row", "loop"))
    return jax.shard_map(
        functools.partial(on_device, 32), mesh=mesh, in_specs=(spec,) * 5, out_specs=spec, check_vma=False
    )
```

```python
import functools
import math

import jax
import jax.numpy as jnp
from jax import lax
from jax.experimental import pallas as pl
from jax.experimental.pallas import tpu as pltpu
from jax.sharding import PartitionSpec as P

WAVENUM = 2.0 * math.pi * 6000.0 / 1500.0
TURNS = WAVENUM / (2.0 * math.pi)
PAIR_SCALE = WAVENUM**3 / (4.0 * math.pi * TURNS)
F32 = jnp.float32
BF16 = jnp.bfloat16
TI = 256
TJ = 256
SUB = 16
LANE = 128
WIDE = 256

SIN_C = None
COS_C = None


def _fit(fn, odd, terms):
    import numpy as np

    nodes = 0.5 * np.cos(np.pi * (np.arange(400) + 0.5) / 400)
    cols = np.stack([nodes ** (2 * n + odd) for n in range(terms)], axis=1)
    coef = np.linalg.lstsq(cols, fn(nodes), rcond=None)[0]
    return [float(np.float32(c)) for c in coef]


def _tables():
    import numpy as np

    s = _fit(lambda t: math.sqrt(2.0) * np.sin(np.pi * t), 1, 4)
    c = _fit(lambda t: math.sqrt(2.0) * np.cos(np.pi * t), 0, 5)
    return s, c


SIN_C, COS_C = _tables()


def horner(coef, y):
    acc = coef[-1] * y + coef[-2]
    for c in coef[-3::-1]:
        acc = acc * y + c
    return acc


def hi_part(x):
    return x.astype(BF16).astype(F32)


def split3(x):
    one = hi_part(x)
    rest = x - one
    two = hi_part(rest)
    return one, two, rest - two


SPLIT_PAIRS = ((0, 0), (0, 1), (1, 0), (0, 2), (2, 0), (1, 1), (1, 2), (2, 1))


def rows8(x, n, a, b):
    return jnp.concatenate([x, n, a, b], axis=0)


def target_rows(geo, center):
    x = (geo[0:3] - center) * TURNS
    m = geo[3:6] * (1.0 / WAVENUM)
    ones = jnp.ones_like(x[0:1])
    xm = jnp.sum(x * m, axis=0, keepdims=True)
    return x, m, split3(rows8(x, m, ones, xm))


def target_table(adj, rows):
    hi = hi_part(adj)
    lo = adj - hi
    return jnp.concatenate([rows[a] for a, _ in SPLIT_PAIRS] + [hi, hi, lo], axis=0)


def source_rows(geo, center):
    x = (geo[0:3] - center) * TURNS
    n = geo[3:6]
    return x, n


def source_table(geo, fwd, x, n):
    area = geo[6:7]
    scaled = fwd * (area * PAIR_SCALE)
    re, im = scaled[0:32], scaled[32:64]
    real = jnp.concatenate([re, im], axis=0)
    imag = jnp.concatenate([im, -re], axis=0)
    rh, ih = hi_part(real), hi_part(imag)
    zero3 = jnp.zeros_like(x)
    zero1 = jnp.zeros_like(x[0:1])
    ones = jnp.ones_like(zero1)
    xn = jnp.sum(x * n, axis=0, keepdims=True)
    prow = split3(rows8(-n, zero3, xn, zero1))
    qrow = split3(rows8(zero3, -x, zero1, ones))
    zeros = jnp.zeros((64, x.shape[1]), F32)
    cols = [
        jnp.concatenate([zeros, rh, real - rh, rh], axis=0),
        jnp.concatenate([zeros, ih, imag - ih, ih], axis=0),
        jnp.concatenate([prow[b] for _, b in SPLIT_PAIRS] + [zeros], axis=0),
        jnp.concatenate([qrow[b] for _, b in SPLIT_PAIRS] + [zeros], axis=0),
    ]
    return cols


def pair_chunk(prod, xi, xj, area):
    wr, wi, pn, q = prod
    d0, d1, d2 = xi[0] - xj[0], xi[1] - xj[1], xi[2] - xj[2]
    r2 = (d0 * d0 + d1 * d1) + (d2 * d2 + area)
    rs = lax.rsqrt(r2)
    turns = r2 * rs
    t = turns - jnp.round(turns)
    v = rs * (1.0 / (2.0 * math.pi))
    y = t * t
    sv = (t * v) * horner(SIN_C, y)
    cv = v * horner(COS_C, y)
    es = sv * cv
    ec = v * v - sv * sv
    yr = ec * wr - es * wi
    yi = ec * wi + es * wr
    a = yi + v * yr
    b = yr - v * yi
    c = rs * ((q * yi - pn * yr) + (3.0 * v) * (pn * a + q * b))
    return a, b, c


def dot(a, b, dims=(((1,), (0,)), ((), ()))):
    return lax.dot_general(a, b, dims, preferred_element_type=F32)


def sum_splits(x):
    return x[0:8] + x[8:16] + x[16:24]


NT = (((1,), (1,)), ((), ()))


def sum_rows(x, n):
    width = x.shape[1]
    zero = jnp.zeros((1, width), F32)
    x1, x2, x3 = split3(x)
    n1 = hi_part(n)
    xr = jnp.concatenate([x1, jnp.ones_like(zero), x2, zero, x3, zero], axis=0)
    nr = jnp.concatenate([n1, zero, n - n1, zero], axis=0)
    z12, z20 = jnp.zeros((12, width), F32), jnp.zeros((20, width), F32)
    rows = ([xr, z20], [z12, nr, z12], [z20, xr])
    return [jnp.concatenate(r, axis=0).astype(BF16) for r in rows]


def read_sums(acc):
    return acc[0:4] + acc[4:8] + acc[8:12], acc[12:15] + acc[16:19], acc[20:24] + acc[24:28] + acc[28:32]


def build_targets(geo, adj, center, cols, left, xi_ref, frow):
    x, m, rows = target_rows(geo, center)
    left[cols, :] = target_table(adj, rows).T.astype(BF16)
    sums = sum_rows(x, m)
    for k in range(3):
        frow[k, :, cols] = sums[k]
    xt = jnp.concatenate([x, m, m[0:2]], axis=0).T
    for k in range(3):
        xi_ref[k, cols, :] = jnp.broadcast_to(xt[:, k : k + 1], (x.shape[1], LANE))


def build_sources(geo, fwd, center, cols, right, rightn, xj_ref, fcol):
    x, n = source_rows(geo, center)
    xj_ref[:, cols] = jnp.concatenate([x, geo[6:7] * (TURNS * TURNS)] * 2, axis=0)
    tab = source_table(geo, fwd, x, n)
    for k in range(2):
        right[k, :, cols] = tab[k].astype(BF16)
        rightn[k, :, cols] = tab[k + 2].astype(BF16)
    sums = sum_rows(x, n)
    for k, part in enumerate((sums[1], sums[0], sums[2])):
        fcol[k, :, cols] = part


def center_of(geo):
    return jnp.round(jnp.mean(geo[0:3], axis=1, keepdims=True))


def run_tiles(count, place, left, right, rightn, xi_ref, xj_ref, frow, fcol, prod, abc, tsum, ssum):
    def start(t):
        i0, j0 = place(t)
        return pl.multiple_of(i0, TI), pl.multiple_of(j0, TJ)

    def products(t, slot):
        i0, j0 = start(t)

        def piece(k):
            if k < 2:
                prod[slot, k] = dot(left[pl.ds(i0, TI), :], right[k, :, pl.ds(j0, TJ)])
            else:
                prod[slot, k] = dot(left[pl.ds(i0, TI), 0:128], rightn[k - 2, :, pl.ds(j0, TJ)])

        return [functools.partial(piece, k) for k in range(4)]

    def values(t, slot):
        i0, j0 = start(t)

        def piece(jj, ii):
            lanes = pl.ds(j0 + jj * WIDE, WIDE)
            here = slice(jj * WIDE, (jj + 1) * WIDE)
            xj = [xj_ref[k : k + 1, lanes] for k in range(4)]
            rows = pl.ds(ii * SUB, SUB)
            xi = [xi_ref[k, pl.ds(i0 + ii * SUB, SUB), :] for k in range(3)]
            xi = [jnp.concatenate([v, v], axis=1) for v in xi]
            pr = [prod[slot, k, rows, here] for k in range(4)]
            a, b, c = pair_chunk(pr, xi, xj[0:3], xj[3])
            for k, val in ((0, a), (2, c)):
                hi = val.astype(BF16)
                abc[slot, k, rows, here] = hi
                abc[slot, k + 1, rows, here] = (val - hi.astype(F32)).astype(BF16)
            abc[slot, 4, rows, here] = b.astype(BF16)

        return [functools.partial(piece, jj, ii) for jj in range(TJ // WIDE) for ii in range(TI // SUB)]

    def sums(t, slot):
        i0, j0 = start(t)
        kept = [None, None]

        def piece(n, k, parts):
            fi = frow[k, :, pl.ds(i0, TI)]
            add = dot(
                jnp.concatenate([fi] * len(parts), axis=1),
                jnp.concatenate([abc[slot, p] for p in parts], axis=0),
            )
            kept[0] = add if n == 0 else kept[0] + add
            if n == 2:
                ssum[:, pl.ds(j0, TJ)] += kept[0]

        def other(n, k, parts):
            fj = fcol[k, :, pl.ds(j0, TJ)]
            add = dot(
                jnp.concatenate([fj] * len(parts), axis=1),
                jnp.concatenate([abc[slot, p] for p in parts], axis=1),
                NT,
            )
            kept[1] = add if n == 0 else kept[1] + add
            if n == 2:
                tsum[:, pl.ds(i0, TI)] += kept[1]

        groups = ((0, (0, 1)), (2, (2, 3)), (1, (4,)))
        return [functools.partial(f, n, *g) for f in (piece, other) for n, g in enumerate(groups)]

    def interleave(vector, matrix):
        gap = max(1, len(vector) // len(matrix))
        for n, todo in enumerate(vector):
            if n % gap == 0 and n // gap < len(matrix):
                matrix[n // gap]()
            todo()

    last = count - 1
    for todo in products(0, 0):
        todo()
    abc[1] = jnp.zeros_like(abc[1])

    def double(u, _):
        t = 2 * u
        interleave(values(t, 0), products(t + 1, 1) + sums(jnp.maximum(t - 1, 0), 1))
        interleave(values(t + 1, 1), products(jnp.minimum(t + 2, last), 0) + sums(t, 0))
        return 0

    lax.fori_loop(0, count // 2, double, 0)
    for todo in sums(last, 1):
        todo()


def pack_kernel(geo, adj, fwd, own, wt, tpack, spack, geo_v, own_v, wt_v, sems):
    copies = [
        pltpu.make_async_copy(src, dst, sems.at[k])
        for k, (src, dst) in enumerate(
            ((adj, tpack.at[0:64]), (fwd, spack.at[0:64]), (geo, geo_v), (own, own_v), (wt, wt_v))
        )
    ]
    for c in copies:
        c.start()
    for c in copies[2:]:
        c.wait()
    geo_rows = jnp.concatenate([geo_v[...], jnp.zeros_like(geo_v[0:1])], axis=0)
    own_rows = jnp.concatenate([wt_v[...], own_v[...].astype(F32)], axis=0)
    for pack in (tpack, spack):
        pack[64:72] = geo_rows
        pack[72:80] = own_rows
    for c in copies[:2]:
        c.wait()


def own_kernel(geo_ref, adj, fwd, left, right, rightn, xi_ref, tsum, ssum, xj_ref, frow, fcol, prod, abc):
    width = geo_ref.shape[1]
    geo = geo_ref[...]
    center = center_of(geo)
    cols = pl.ds(0, width)
    build_targets(geo, adj[...], center, cols, left, xi_ref, frow)
    build_sources(geo, fwd[...], center, cols, right, rightn, xj_ref, fcol)
    tsum[...] = jnp.zeros_like(tsum)
    ssum[...] = jnp.zeros_like(ssum)
    n_j = width // TJ
    run_tiles(
        (width // TI) * n_j, lambda t: ((t // n_j) * TI, lax.rem(t, n_j) * TJ),
        left, right, rightn, xi_ref, xj_ref, frow, fcol, prod, abc, tsum, ssum,
    )


def reverse_bits(x, bits):
    out = jnp.zeros_like(x)
    for b in range(bits):
        out = out | (((x >> b) & 1) << (bits - 1 - b))
    return out


def rest_kernel(
    tpack, far, near, left_o, right_o, rightn_o, xi_o, tsum_o, ssum_o,
    out_ref,
    left, right, rightn, xi_ref, xj_ref, frow, fcol, prod, abc, tsum, ssum,
):
    width = tpack.shape[1]
    geo = tpack[64:71]
    center = center_of(geo)
    first, second = pl.ds(0, width), pl.ds(width, width)
    left[first, :] = left_o[...]
    right[:, :, first] = right_o[...]
    rightn[:, :, first] = rightn_o[...]
    xi_ref[:, first, :] = xi_o[...]
    x, n = source_rows(geo, center)
    tsums, ssums = sum_rows(x, n * (1.0 / WAVENUM)), sum_rows(x, n)
    for k in range(3):
        frow[k, :, first] = tsums[k]
        fcol[k, :, first] = ssums[(1, 0, 2)[k]]
    xj_ref[:, first] = jnp.concatenate([x, geo[6:7] * (TURNS * TURNS)] * 2, axis=0)
    tsum[:, first] = tsum_o[...]
    ssum[:, first] = ssum_o[...]
    tsum[:, second] = jnp.zeros_like(tsum_o)
    ssum[:, second] = jnp.zeros_like(ssum_o)
    build_targets(far[64:71], far[0:64], center, second, left, xi_ref, frow)
    build_sources(near[64:71], near[0:64], center, second, right, rightn, xj_ref, fcol)

    n_i, n_j = width // TI, width // TJ
    block = n_i * n_j

    def place(t):
        b = t // block
        inner = lax.rem(t, block)
        i0 = jnp.where(b > 0, width, 0) + (inner // n_j) * TI
        j0 = jnp.where(b == 1, 0, width) + lax.rem(inner, n_j) * TJ
        return i0, j0

    run_tiles(3 * block, place, left, right, rightn, xi_ref, xj_ref, frow, fcol, prod, abc, tsum, ssum)

    def target_grad(g, cols):
        x = (g[0:3] - center) * TURNS
        m = g[3:6] * (1.0 / WAVENUM)
        sb, an, sc = read_sums(tsum[:, cols])
        gx = (2.0 * math.pi) * (x * sc[3:4] - sc[0:3]) + an - m * sb[3:4]
        gn = sb[0:3] - x * sb[3:4]
        return gx * TURNS, gn * (1.0 / WAVENUM)

    def source_grad(g, cols):
        x = (g[0:3] - center) * TURNS
        n = g[3:6]
        sa, bm, sc = read_sums(ssum[:, cols])
        gx = (2.0 * math.pi) * (x * sc[3:4] - sc[0:3]) - n * sa[3:4] + bm
        gn = sa[0:3] - x * sa[3:4]
        return gx * TURNS, gn

    t_own, s_own = target_grad(geo, first), source_grad(geo, first)
    zero2 = jnp.zeros((2, width), F32)
    grads = [
        (t_own[0] + s_own[0], t_own[1] + s_own[1]),
        target_grad(far[64:71], second),
        source_grad(near[64:71], second),
    ]
    slots, _, cp_dev = out_ref.shape
    low_iota = lax.broadcasted_iota(jnp.int32, (cp_dev, width), 0)
    terms = []
    for (gx, gn), pack in zip(grads, (tpack, far, near)):
        g = jnp.concatenate([gx, gn, zero2], axis=0)
        own, wt = pack[76:80].astype(jnp.int32), pack[72:76]
        place_of = reverse_bits(own // cp_dev, slots.bit_length() - 1)
        low = lax.rem(own, cp_dev)
        for s in range(4):
            gw = g * wt[s : s + 1]
            hi = hi_part(gw)
            here = jnp.where(low[s : s + 1] == low_iota, 1.0, 0.0).astype(BF16)
            both = jnp.concatenate([hi, gw - hi], axis=0).astype(BF16)
            where_to = jnp.broadcast_to(place_of[s : s + 1].astype(F32), both.shape).astype(BF16)
            terms.append((where_to, both, here))
    onehot = jnp.concatenate([t[2] for t in terms], axis=1)
    where_to = jnp.concatenate([t[0] for t in terms], axis=1)
    both = jnp.concatenate([t[1] for t in terms], axis=1)

    def add_owner(s0):
        rows = [jnp.where(where_to == (s0 + r), both, jnp.zeros_like(both)) for r in range(16)]
        acc = dot(jnp.concatenate(rows, axis=0), onehot, NT).reshape(16, 16, cp_dev)
        out_ref[s0 : s0 + 16] = acc[:, 0:8] + acc[:, 8:16]

    for s0 in range(0, slots, 16):
        add_owner(s0)


def shape(dims, kind):
    return jax.ShapeDtypeStruct(dims, kind)


def tile_scratch():
    return [pltpu.VMEM((2, 4, TI, TJ), F32), pltpu.VMEM((2, 5, TI, TJ), BF16)]


PARAMS = pltpu.CompilerParams(vmem_limit_bytes=20 * 1024 * 1024)


def pack_call(geo, adj, fwd, own, wt):
    width = geo.shape[1]
    return pl.pallas_call(
        pack_kernel,
        in_specs=[pl.BlockSpec(memory_space=pl.ANY)] * 5,
        out_shape=[shape((80, width), F32)] * 2,
        scratch_shapes=[
            pltpu.VMEM((7, width), F32), pltpu.VMEM((4, width), jnp.int32), pltpu.VMEM((4, width), F32),
            pltpu.SemaphoreType.DMA((5,)),
        ],
        name="pack",
    )(geo, adj, fwd, own, wt)


def own_call(geo, adj, fwd):
    width = geo.shape[1]
    return pl.pallas_call(
        own_kernel,
        out_shape=[
            shape((width, 256), BF16), shape((2, 256, width), BF16), shape((2, 128, width), BF16),
            shape((3, width, LANE), F32),
            shape((32, width), F32), shape((32, width), F32),
        ],
        scratch_shapes=[
            pltpu.VMEM((8, width), F32), pltpu.VMEM((3, 32, width), BF16), pltpu.VMEM((3, 32, width), BF16)
        ]
        + tile_scratch(),
        compiler_params=PARAMS,
        cost_estimate=pl.CostEstimate(flops=4 * 10**9, bytes_accessed=4 * 10**6, transcendentals=0),
        name="own",
    )(geo, adj, fwd)


def rest_call(args, slots, cp_dev):
    width = args[0].shape[1]
    total = 2 * width
    return pl.pallas_call(
        rest_kernel,
        out_shape=shape((slots, 8, cp_dev), F32),
        scratch_shapes=[
            pltpu.VMEM((total, 256), BF16),
            pltpu.VMEM((2, 256, total), BF16),
            pltpu.VMEM((2, 128, total), BF16),
            pltpu.VMEM((3, total, LANE), F32),
            pltpu.VMEM((8, total), F32),
            pltpu.VMEM((3, 32, total), BF16),
            pltpu.VMEM((3, 32, total), BF16),
        ]
        + tile_scratch()
        + [pltpu.VMEM((32, total), F32), pltpu.VMEM((32, total), F32)],
        compiler_params=PARAMS,
        cost_estimate=pl.CostEstimate(flops=12 * 10**9, bytes_accessed=4 * 10**6, transcendentals=0),
        name="rest",
    )(*args)


def swap(x, axis, bit):
    size = lax.axis_size(axis)
    return lax.ppermute(x, axis, [(k, k ^ bit) for k in range(size)])


def halving(cur):
    n_loop = lax.axis_size("loop").bit_length() - 1
    n_row = lax.axis_size("row").bit_length() - 1
    steps = [("loop", 1 << b) for b in range(n_loop)] + [("row", 1 << b) for b in range(n_row)]
    for axis, bit in steps:
        half = cur.shape[0] // 2
        up = jnp.where((lax.axis_index(axis) & bit) > 0, 1, 0)
        keep = lax.dynamic_slice_in_dim(cur, up * half, half, 0)
        send = lax.dynamic_slice_in_dim(cur, (1 - up) * half, half, 0)
        cur = keep + swap(send, axis, bit)
    return cur[0, 0:6]


def on_device(cp_dev, geometry, adjoint, forward, owner_map, owner_weight):
    slots = lax.axis_size("row") * lax.axis_size("loop")
    tpack, spack = pack_call(geometry, adjoint, forward, owner_map, owner_weight)
    far = swap(tpack, "loop", 2)
    near = swap(spack, "loop", 1)
    tables = own_call(geometry, adjoint, forward)
    return halving(rest_call((tpack, far, near, *tables), slots, cp_dev))


def solution(mesh):
    spec = P(None, ("parts", "row", "loop"))
    return jax.shard_map(
        functools.partial(on_device, 32), mesh=mesh, in_specs=(spec,) * 5, out_specs=spec, check_vma=False
    )
```

```python
import functools
import math

import jax
import jax.numpy as jnp
from jax import lax
from jax.experimental import pallas as pl
from jax.experimental.pallas import tpu as pltpu
from jax.sharding import PartitionSpec as P

WAVENUM = 2.0 * math.pi * 6000.0 / 1500.0
TURNS = WAVENUM / (2.0 * math.pi)
PAIR_SCALE = WAVENUM**3 / (4.0 * math.pi * TURNS)
F32 = jnp.float32
BF16 = jnp.bfloat16
TI = 256
TJ = 256
SUB = 16
STEP = 8
LANE = 128
WIDE = 256

SIN_C = None
COS_C = None


def _fit(fn, odd, terms):
    import numpy as np

    nodes = 0.5 * np.cos(np.pi * (np.arange(400) + 0.5) / 400)
    cols = np.stack([nodes ** (2 * n + odd) for n in range(terms)], axis=1)
    coef = np.linalg.lstsq(cols, fn(nodes), rcond=None)[0]
    return [float(np.float32(c)) for c in coef]


def _tables():
    import numpy as np

    s = _fit(lambda t: math.sqrt(2.0) * np.sin(np.pi * t), 1, 4)
    c = _fit(lambda t: math.sqrt(2.0) * np.cos(np.pi * t), 0, 5)
    return s, c


SIN_C, COS_C = _tables()


def horner(coef, y):
    acc = coef[-1] * y + coef[-2]
    for c in coef[-3::-1]:
        acc = acc * y + c
    return acc


def hi_part(x):
    return x.astype(BF16).astype(F32)


def split3(x):
    one = hi_part(x)
    rest = x - one
    two = hi_part(rest)
    return one, two, rest - two


SPLIT_PAIRS = ((0, 0), (0, 1), (1, 0), (0, 2), (2, 0), (1, 1), (1, 2), (2, 1))


def rows8(x, n, a, b):
    return jnp.concatenate([x, n, a, b], axis=0)


def target_rows(geo, center):
    x = (geo[0:3] - center) * TURNS
    m = geo[3:6] * (1.0 / WAVENUM)
    ones = jnp.ones_like(x[0:1])
    xm = jnp.sum(x * m, axis=0, keepdims=True)
    return x, m, split3(rows8(x, m, ones, xm))


def target_table(adj, rows):
    hi = hi_part(adj)
    lo = adj - hi
    return jnp.concatenate([rows[a] for a, _ in SPLIT_PAIRS] + [hi, hi, lo], axis=0)


def source_rows(geo, center):
    x = (geo[0:3] - center) * TURNS
    n = geo[3:6]
    return x, n


def source_table(geo, fwd, x, n):
    area = geo[6:7]
    scaled = fwd * (area * PAIR_SCALE)
    re, im = scaled[0:32], scaled[32:64]
    real = jnp.concatenate([re, im], axis=0)
    imag = jnp.concatenate([im, -re], axis=0)
    rh, ih = hi_part(real), hi_part(imag)
    zero3 = jnp.zeros_like(x)
    zero1 = jnp.zeros_like(x[0:1])
    ones = jnp.ones_like(zero1)
    xn = jnp.sum(x * n, axis=0, keepdims=True)
    prow = split3(rows8(-n, zero3, xn, zero1))
    qrow = split3(rows8(zero3, -x, zero1, ones))
    zeros = jnp.zeros((64, x.shape[1]), F32)
    cols = [
        jnp.concatenate([zeros, rh, real - rh, rh], axis=0),
        jnp.concatenate([zeros, ih, imag - ih, ih], axis=0),
        jnp.concatenate([prow[b] for _, b in SPLIT_PAIRS] + [zeros], axis=0),
        jnp.concatenate([qrow[b] for _, b in SPLIT_PAIRS] + [zeros], axis=0),
    ]
    return cols


def pair_chunk(prod, xi, xj, area):
    wr, wi, pn, q = prod
    d0, d1, d2 = xi[0] - xj[0], xi[1] - xj[1], xi[2] - xj[2]
    r2 = (d0 * d0 + d1 * d1) + (d2 * d2 + area)
    rs = lax.rsqrt(r2)
    turns = r2 * rs
    t = turns - jnp.round(turns)
    v = rs * (1.0 / (2.0 * math.pi))
    y = t * t
    sv = (t * v) * horner(SIN_C, y)
    cv = v * horner(COS_C, y)
    es = sv * cv
    ec = v * v - sv * sv
    yr = ec * wr - es * wi
    yi = ec * wi + es * wr
    a = yi + v * yr
    b = yr - v * yi
    c = rs * ((q * yi - pn * yr) + (3.0 * v) * (pn * a + q * b))
    return a, b, c


def dot(a, b, dims=(((1,), (0,)), ((), ()))):
    return lax.dot_general(a, b, dims, preferred_element_type=F32)


def sum_splits(x):
    return x[0:8] + x[8:16] + x[16:24]


NT = (((1,), (1,)), ((), ()))


def sum_rows(x, n):
    width = x.shape[1]
    zero = jnp.zeros((1, width), F32)
    x1, x2, x3 = split3(x)
    n1 = hi_part(n)
    xr = jnp.concatenate([x1, jnp.ones_like(zero), x2, zero, x3, zero], axis=0)
    nr = jnp.concatenate([n1, zero, n - n1, zero], axis=0)
    z12, z20 = jnp.zeros((12, width), F32), jnp.zeros((20, width), F32)
    rows = ([xr, z20], [z12, nr, z12], [z20, xr])
    return [jnp.concatenate(r, axis=0).astype(BF16) for r in rows]


def read_sums(acc):
    return acc[0:4] + acc[4:8] + acc[8:12], acc[12:15] + acc[16:19], acc[20:24] + acc[24:28] + acc[28:32]


def build_targets(geo, adj, center, cols, left, xi_ref, frow):
    x, m, rows = target_rows(geo, center)
    left[cols, :] = target_table(adj, rows).T.astype(BF16)
    sums = sum_rows(x, m)
    for k in range(3):
        frow[k, :, cols] = sums[k]
    xt = jnp.concatenate([x, m, m[0:2]], axis=0).T
    for k in range(3):
        xi_ref[k, cols, :] = jnp.broadcast_to(xt[:, k : k + 1], (x.shape[1], LANE))


def build_sources(geo, fwd, center, cols, right, rightn, xj_ref, fcol):
    x, n = source_rows(geo, center)
    xj_ref[:, cols] = jnp.concatenate([x, geo[6:7] * (TURNS * TURNS)] * 2, axis=0)
    tab = source_table(geo, fwd, x, n)
    for k in range(2):
        right[k, :, cols] = tab[k].astype(BF16)
        rightn[k, :, cols] = tab[k + 2].astype(BF16)
    sums = sum_rows(x, n)
    for k, part in enumerate((sums[1], sums[0], sums[2])):
        fcol[k, :, cols] = part


def center_of(geo):
    return jnp.round(jnp.mean(geo[0:3], axis=1, keepdims=True))


def run_tiles(count, place, left, right, rightn, xi_ref, xj_ref, frow, fcol, prod, abc, tsum, ssum):
    def start(t):
        i0, j0 = place(t)
        return pl.multiple_of(i0, TI), pl.multiple_of(j0, TJ)

    def products(t, slot):
        i0, j0 = start(t)

        def piece(k):
            if k < 2:
                prod[slot, k] = dot(left[pl.ds(i0, TI), :], right[k, :, pl.ds(j0, TJ)])
            else:
                prod[slot, k] = dot(left[pl.ds(i0, TI), 0:128], rightn[k - 2, :, pl.ds(j0, TJ)])

        return [functools.partial(piece, k) for k in range(4)]

    def values(t, slot):
        i0, j0 = start(t)

        def piece(jj, ii):
            lanes = pl.ds(j0 + jj * WIDE, WIDE)
            here = slice(jj * WIDE, (jj + 1) * WIDE)
            xj = [xj_ref[k : k + 1, lanes] for k in range(4)]
            rows = pl.ds(ii * SUB, SUB)
            halves = []
            for r in range(0, SUB, STEP):
                xi = [xi_ref[k, pl.ds(i0 + ii * SUB + r, STEP), :] for k in range(3)]
                xi = [jnp.concatenate([v, v], axis=1) for v in xi]
                pr = [prod[slot, k, pl.ds(ii * SUB + r, STEP), here] for k in range(4)]
                halves.append(pair_chunk(pr, xi, xj[0:3], xj[3]))
            a, b, c = [jnp.concatenate(parts, axis=0) for parts in zip(*halves)]
            for k, val in ((0, a), (2, c)):
                hi = val.astype(BF16)
                abc[slot, k, rows, here] = hi
                abc[slot, k + 1, rows, here] = (val - hi.astype(F32)).astype(BF16)
            abc[slot, 4, rows, here] = b.astype(BF16)

        return [functools.partial(piece, jj, ii) for jj in range(TJ // WIDE) for ii in range(TI // SUB)]

    def sums(t, slot):
        i0, j0 = start(t)
        kept = [None, None]
        groups = ((0, (0,)), (0, (1,)), (2, (2,)), (2, (3,)), (1, (4,)))

        def piece(n, k, parts):
            fi = frow[k, :, pl.ds(i0, TI)]
            add = dot(
                jnp.concatenate([fi] * len(parts), axis=1),
                jnp.concatenate([abc[slot, p] for p in parts], axis=0),
            )
            kept[0] = add if n == 0 else kept[0] + add
            if n == len(groups) - 1:
                ssum[:, pl.ds(j0, TJ)] += kept[0]

        def other(n, k, parts):
            fj = fcol[k, :, pl.ds(j0, TJ)]
            add = dot(
                jnp.concatenate([fj] * len(parts), axis=1),
                jnp.concatenate([abc[slot, p] for p in parts], axis=1),
                NT,
            )
            kept[1] = add if n == 0 else kept[1] + add
            if n == len(groups) - 1:
                tsum[:, pl.ds(i0, TI)] += kept[1]

        return [functools.partial(f, n, *g) for n, g in enumerate(groups) for f in (piece, other)]

    def interleave(vector, matrix):
        done = 0
        for n, todo in enumerate(vector):
            while done < len(matrix) and done * len(vector) <= n * len(matrix):
                matrix[done]()
                done += 1
            todo()

    last = count - 1
    for todo in products(0, 0):
        todo()
    abc[1] = jnp.zeros_like(abc[1])

    def double(u, _):
        t = 2 * u
        def half(h, _):
            @pl.when(h == 0)
            def _():
                interleave(values(t, 0), products(t + 1, 1) + sums(jnp.maximum(t - 1, 0), 1))

            @pl.when(h == 1)
            def _():
                interleave(values(t + 1, 1), products(jnp.minimum(t + 2, last), 0) + sums(t, 0))

            return 0

        lax.fori_loop(0, 2, half, 0)
        return 0

    lax.fori_loop(0, count // 2, double, 0)
    for todo in sums(last, 1):
        todo()


def pack_kernel(geo, adj, fwd, own, wt, tpack, spack, geo_v, own_v, wt_v, sems):
    copies = [
        pltpu.make_async_copy(src, dst, sems.at[k])
        for k, (src, dst) in enumerate(
            ((adj, tpack.at[0:64]), (fwd, spack.at[0:64]), (geo, geo_v), (own, own_v), (wt, wt_v))
        )
    ]
    for c in copies:
        c.start()
    for c in copies[2:]:
        c.wait()
    geo_rows = jnp.concatenate([geo_v[...], jnp.zeros_like(geo_v[0:1])], axis=0)
    own_rows = jnp.concatenate([wt_v[...], own_v[...].astype(F32)], axis=0)
    for pack in (tpack, spack):
        pack[64:72] = geo_rows
        pack[72:80] = own_rows
    for c in copies[:2]:
        c.wait()


def own_kernel(geo_ref, adj, fwd, left, right, rightn, xi_ref, tsum, ssum, xj_ref, frow, fcol, prod, abc):
    width = geo_ref.shape[1]
    geo = geo_ref[...]
    center = center_of(geo)
    cols = pl.ds(0, width)
    build_targets(geo, adj[...], center, cols, left, xi_ref, frow)
    build_sources(geo, fwd[...], center, cols, right, rightn, xj_ref, fcol)
    tsum[...] = jnp.zeros_like(tsum)
    ssum[...] = jnp.zeros_like(ssum)
    n_j = width // TJ
    run_tiles(
        (width // TI) * n_j, lambda t: ((t // n_j) * TI, lax.rem(t, n_j) * TJ),
        left, right, rightn, xi_ref, xj_ref, frow, fcol, prod, abc, tsum, ssum,
    )


def reverse_bits(x, bits):
    out = jnp.zeros_like(x)
    for b in range(bits):
        out = out | (((x >> b) & 1) << (bits - 1 - b))
    return out


def rest_kernel(
    tpack, far, near, left_o, right_o, rightn_o, xi_o, tsum_o, ssum_o,
    out_ref,
    left, right, rightn, xi_ref, xj_ref, frow, fcol, prod, abc, tsum, ssum,
):
    width = tpack.shape[1]
    geo = tpack[64:71]
    center = center_of(geo)
    first, second = pl.ds(0, width), pl.ds(width, width)
    left[first, :] = left_o[...]
    right[:, :, first] = right_o[...]
    rightn[:, :, first] = rightn_o[...]
    xi_ref[:, first, :] = xi_o[...]
    x, n = source_rows(geo, center)
    tsums, ssums = sum_rows(x, n * (1.0 / WAVENUM)), sum_rows(x, n)
    for k in range(3):
        frow[k, :, first] = tsums[k]
        fcol[k, :, first] = ssums[(1, 0, 2)[k]]
    xj_ref[:, first] = jnp.concatenate([x, geo[6:7] * (TURNS * TURNS)] * 2, axis=0)
    tsum[:, first] = tsum_o[...]
    ssum[:, first] = ssum_o[...]
    tsum[:, second] = jnp.zeros_like(tsum_o)
    ssum[:, second] = jnp.zeros_like(ssum_o)
    build_targets(far[64:71], far[0:64], center, second, left, xi_ref, frow)
    build_sources(near[64:71], near[0:64], center, second, right, rightn, xj_ref, fcol)

    n_i, n_j = width // TI, width // TJ
    block = n_i * n_j

    def place(t):
        b = t // block
        inner = lax.rem(t, block)
        i0 = jnp.where(b > 0, width, 0) + (inner // n_j) * TI
        j0 = jnp.where(b == 1, 0, width) + lax.rem(inner, n_j) * TJ
        return i0, j0

    run_tiles(3 * block, place, left, right, rightn, xi_ref, xj_ref, frow, fcol, prod, abc, tsum, ssum)

    def target_grad(g, cols):
        x = (g[0:3] - center) * TURNS
        m = g[3:6] * (1.0 / WAVENUM)
        sb, an, sc = read_sums(tsum[:, cols])
        gx = (2.0 * math.pi) * (x * sc[3:4] - sc[0:3]) + an - m * sb[3:4]
        gn = sb[0:3] - x * sb[3:4]
        return gx * TURNS, gn * (1.0 / WAVENUM)

    def source_grad(g, cols):
        x = (g[0:3] - center) * TURNS
        n = g[3:6]
        sa, bm, sc = read_sums(ssum[:, cols])
        gx = (2.0 * math.pi) * (x * sc[3:4] - sc[0:3]) - n * sa[3:4] + bm
        gn = sa[0:3] - x * sa[3:4]
        return gx * TURNS, gn

    t_own, s_own = target_grad(geo, first), source_grad(geo, first)
    zero2 = jnp.zeros((2, width), F32)
    grads = [
        (t_own[0] + s_own[0], t_own[1] + s_own[1]),
        target_grad(far[64:71], second),
        source_grad(near[64:71], second),
    ]
    slots, _, cp_dev = out_ref.shape
    low_iota = lax.broadcasted_iota(jnp.int32, (cp_dev, width), 0)
    terms = []
    for (gx, gn), pack in zip(grads, (tpack, far, near)):
        g = jnp.concatenate([gx, gn, zero2], axis=0)
        own, wt = pack[76:80].astype(jnp.int32), pack[72:76]
        place_of = reverse_bits(own // cp_dev, slots.bit_length() - 1)
        low = lax.rem(own, cp_dev)
        for s in range(4):
            gw = g * wt[s : s + 1]
            hi = hi_part(gw)
            here = jnp.where(low[s : s + 1] == low_iota, 1.0, 0.0).astype(BF16)
            both = jnp.concatenate([hi, gw - hi], axis=0).astype(BF16)
            where_to = jnp.broadcast_to(place_of[s : s + 1].astype(F32), both.shape).astype(BF16)
            terms.append((where_to, both, here))
    onehot = jnp.concatenate([t[2] for t in terms], axis=1)
    where_to = jnp.concatenate([t[0] for t in terms], axis=1)
    both = jnp.concatenate([t[1] for t in terms], axis=1)

    def add_owner(s0):
        rows = [jnp.where(where_to == (s0 + r), both, jnp.zeros_like(both)) for r in range(16)]
        acc = dot(jnp.concatenate(rows, axis=0), onehot, NT).reshape(16, 16, cp_dev)
        out_ref[s0 : s0 + 16] = acc[:, 0:8] + acc[:, 8:16]

    for s0 in range(0, slots, 16):
        add_owner(s0)


def shape(dims, kind):
    return jax.ShapeDtypeStruct(dims, kind)


def tile_scratch():
    return [pltpu.VMEM((2, 4, TI, TJ), F32), pltpu.VMEM((2, 5, TI, TJ), BF16)]


PARAMS = pltpu.CompilerParams(vmem_limit_bytes=20 * 1024 * 1024)


def pack_call(geo, adj, fwd, own, wt):
    width = geo.shape[1]
    return pl.pallas_call(
        pack_kernel,
        in_specs=[pl.BlockSpec(memory_space=pl.ANY)] * 5,
        out_shape=[shape((80, width), F32)] * 2,
        scratch_shapes=[
            pltpu.VMEM((7, width), F32), pltpu.VMEM((4, width), jnp.int32), pltpu.VMEM((4, width), F32),
            pltpu.SemaphoreType.DMA((5,)),
        ],
        name="pack",
    )(geo, adj, fwd, own, wt)


def own_call(geo, adj, fwd):
    width = geo.shape[1]
    return pl.pallas_call(
        own_kernel,
        out_shape=[
            shape((width, 256), BF16), shape((2, 256, width), BF16), shape((2, 128, width), BF16),
            shape((3, width, LANE), F32),
            shape((32, width), F32), shape((32, width), F32),
        ],
        scratch_shapes=[
            pltpu.VMEM((8, width), F32), pltpu.VMEM((3, 32, width), BF16), pltpu.VMEM((3, 32, width), BF16)
        ]
        + tile_scratch(),
        compiler_params=PARAMS,
        cost_estimate=pl.CostEstimate(flops=4 * 10**9, bytes_accessed=4 * 10**6, transcendentals=0),
        name="own",
    )(geo, adj, fwd)


def rest_call(args, slots, cp_dev):
    width = args[0].shape[1]
    total = 2 * width
    return pl.pallas_call(
        rest_kernel,
        out_shape=shape((slots, 8, cp_dev), F32),
        scratch_shapes=[
            pltpu.VMEM((total, 256), BF16),
            pltpu.VMEM((2, 256, total), BF16),
            pltpu.VMEM((2, 128, total), BF16),
            pltpu.VMEM((3, total, LANE), F32),
            pltpu.VMEM((8, total), F32),
            pltpu.VMEM((3, 32, total), BF16),
            pltpu.VMEM((3, 32, total), BF16),
        ]
        + tile_scratch()
        + [pltpu.VMEM((32, total), F32), pltpu.VMEM((32, total), F32)],
        compiler_params=PARAMS,
        cost_estimate=pl.CostEstimate(flops=12 * 10**9, bytes_accessed=4 * 10**6, transcendentals=0),
        name="rest",
    )(*args)


def swap(x, axis, bit):
    size = lax.axis_size(axis)
    return lax.ppermute(x, axis, [(k, k ^ bit) for k in range(size)])


def halving(cur):
    n_loop = lax.axis_size("loop").bit_length() - 1
    n_row = lax.axis_size("row").bit_length() - 1
    steps = [("loop", 1 << b) for b in range(n_loop)] + [("row", 1 << b) for b in range(n_row)]
    for axis, bit in steps:
        half = cur.shape[0] // 2
        up = jnp.where((lax.axis_index(axis) & bit) > 0, 1, 0)
        keep = lax.dynamic_slice_in_dim(cur, up * half, half, 0)
        send = lax.dynamic_slice_in_dim(cur, (1 - up) * half, half, 0)
        cur = keep + swap(send, axis, bit)
    return cur[0, 0:6]


def on_device(cp_dev, geometry, adjoint, forward, owner_map, owner_weight):
    slots = lax.axis_size("row") * lax.axis_size("loop")
    tpack, spack = pack_call(geometry, adjoint, forward, owner_map, owner_weight)
    far = swap(tpack, "loop", 2)
    near = swap(spack, "loop", 1)
    tables = own_call(geometry, adjoint, forward)
    return halving(rest_call((tpack, far, near, *tables), slots, cp_dev))


def solution(mesh):
    spec = P(None, ("parts", "row", "loop"))
    return jax.shard_map(
        functools.partial(on_device, 32), mesh=mesh, in_specs=(spec,) * 5, out_specs=spec, check_vma=False
    )
```

```python
import functools
import math

import jax
import jax.numpy as jnp
from jax import lax
from jax.experimental import pallas as pl
from jax.experimental.pallas import tpu as pltpu
from jax.sharding import PartitionSpec as P

WAVENUM = 2.0 * math.pi * 6000.0 / 1500.0
TURNS = WAVENUM / (2.0 * math.pi)
PAIR_SCALE = WAVENUM**3 / (4.0 * math.pi * TURNS)
F32 = jnp.float32
BF16 = jnp.bfloat16
TI = 256
TJ = 256
SUB = 16
STEP = 8
LANE = 128
WIDE = 256

SIN_C = None
COS_C = None


def _fit(fn, odd, terms):
    import numpy as np

    nodes = 0.5 * np.cos(np.pi * (np.arange(400) + 0.5) / 400)
    cols = np.stack([nodes ** (2 * n + odd) for n in range(terms)], axis=1)
    coef = np.linalg.lstsq(cols, fn(nodes), rcond=None)[0]
    return [float(np.float32(c)) for c in coef]


def _tables():
    import numpy as np

    s = _fit(lambda t: math.sqrt(2.0) * np.sin(np.pi * t), 1, 4)
    c = _fit(lambda t: math.sqrt(2.0) * np.cos(np.pi * t), 0, 5)
    return s, c


SIN_C, COS_C = _tables()


def horner(coef, y):
    acc = coef[-1] * y + coef[-2]
    for c in coef[-3::-1]:
        acc = acc * y + c
    return acc


def hi_part(x):
    return x.astype(BF16).astype(F32)


def split3(x):
    one = hi_part(x)
    rest = x - one
    two = hi_part(rest)
    return one, two, rest - two


SPLIT_PAIRS = ((0, 0), (0, 1), (1, 0), (0, 2), (2, 0), (1, 1), (1, 2), (2, 1))


def rows8(x, n, a, b):
    return jnp.concatenate([x, n, a, b], axis=0)


def target_rows(geo, center):
    x = (geo[0:3] - center) * TURNS
    m = geo[3:6] * (1.0 / WAVENUM)
    ones = jnp.ones_like(x[0:1])
    xm = jnp.sum(x * m, axis=0, keepdims=True)
    return x, m, split3(rows8(x, m, ones, xm))


def target_table(adj, rows):
    hi = hi_part(adj)
    lo = adj - hi
    return jnp.concatenate([rows[a] for a, _ in SPLIT_PAIRS] + [hi, hi, lo], axis=0)


def source_rows(geo, center):
    x = (geo[0:3] - center) * TURNS
    n = geo[3:6]
    return x, n


def source_table(geo, fwd, x, n):
    area = geo[6:7]
    scaled = fwd * (area * PAIR_SCALE)
    re, im = scaled[0:32], scaled[32:64]
    real = jnp.concatenate([re, im], axis=0)
    imag = jnp.concatenate([im, -re], axis=0)
    rh, ih = hi_part(real), hi_part(imag)
    zero3 = jnp.zeros_like(x)
    zero1 = jnp.zeros_like(x[0:1])
    ones = jnp.ones_like(zero1)
    xn = jnp.sum(x * n, axis=0, keepdims=True)
    prow = split3(rows8(-n, zero3, xn, zero1))
    qrow = split3(rows8(zero3, -x, zero1, ones))
    zeros = jnp.zeros((64, x.shape[1]), F32)
    cols = [
        jnp.concatenate([zeros, rh, real - rh, rh], axis=0),
        jnp.concatenate([zeros, ih, imag - ih, ih], axis=0),
        jnp.concatenate([prow[b] for _, b in SPLIT_PAIRS] + [zeros], axis=0),
        jnp.concatenate([qrow[b] for _, b in SPLIT_PAIRS] + [zeros], axis=0),
    ]
    return cols


def pair_chunk(prod, xi, xj, area):
    wr, wi, pn, q = prod
    d0, d1, d2 = xi[0] - xj[0], xi[1] - xj[1], xi[2] - xj[2]
    r2 = (d0 * d0 + d1 * d1) + (d2 * d2 + area)
    rs = lax.rsqrt(r2)
    turns = r2 * rs
    t = turns - jnp.round(turns)
    v = rs * (1.0 / (2.0 * math.pi))
    y = t * t
    sv = (t * v) * horner(SIN_C, y)
    cv = v * horner(COS_C, y)
    es = sv * cv
    ec = v * v - sv * sv
    yr = ec * wr - es * wi
    yi = ec * wi + es * wr
    a = yi + v * yr
    b = yr - v * yi
    c = rs * ((q * yi - pn * yr) + (3.0 * v) * (pn * a + q * b))
    return a, b, c


def dot(a, b, dims=(((1,), (0,)), ((), ()))):
    return lax.dot_general(a, b, dims, preferred_element_type=F32)


def sum_splits(x):
    return x[0:8] + x[8:16] + x[16:24]


NT = (((1,), (1,)), ((), ()))


def sum_rows(x, n):
    width = x.shape[1]
    zero = jnp.zeros((1, width), F32)
    x1, x2, x3 = split3(x)
    n1 = hi_part(n)
    xr = jnp.concatenate([x1, jnp.ones_like(zero), x2, zero, x3, zero], axis=0)
    nr = jnp.concatenate([n1, zero, n - n1, zero], axis=0)
    z12, z20 = jnp.zeros((12, width), F32), jnp.zeros((20, width), F32)
    rows = ([xr, z20], [z12, nr, z12], [z20, xr])
    return [jnp.concatenate(r, axis=0).astype(BF16) for r in rows]


def read_sums(acc):
    return acc[0:4] + acc[4:8] + acc[8:12], acc[12:15] + acc[16:19], acc[20:24] + acc[24:28] + acc[28:32]


def build_targets(geo, adj, center, cols, left, xi_ref, frow):
    x, m, rows = target_rows(geo, center)
    left[cols, :] = target_table(adj, rows).T.astype(BF16)
    sums = sum_rows(x, m)
    for k in range(3):
        frow[k, :, cols] = sums[k]
    row = lax.broadcasted_iota(jnp.int32, (128, 3 * LANE), 0)
    axis = lax.broadcasted_iota(jnp.int32, (128, 3 * LANE), 1) // LANE
    pick = (row == axis) | (row == axis + 16) | (row == axis + 32)
    spread = dot(left[cols, 0:128], jnp.where(pick, 1.0, 0.0).astype(BF16))
    for k in range(3):
        xi_ref[k, cols, :] = spread[:, k * LANE : (k + 1) * LANE]


def build_sources(geo, fwd, center, cols, right, rightn, xj_ref, fcol):
    x, n = source_rows(geo, center)
    xj_ref[:, cols] = jnp.concatenate([x, geo[6:7] * (TURNS * TURNS)] * 2, axis=0)
    tab = source_table(geo, fwd, x, n)
    for k in range(2):
        right[k, :, cols] = tab[k].astype(BF16)
        rightn[k, :, cols] = tab[k + 2].astype(BF16)
    sums = sum_rows(x, n)
    for k, part in enumerate((sums[1], sums[0], sums[2])):
        fcol[k, :, cols] = part


def center_of(geo):
    return jnp.round(jnp.mean(geo[0:3], axis=1, keepdims=True))


def run_tiles(count, place, left, right, rightn, xi_ref, xj_ref, frow, fcol, prod, abc, tsum, ssum):
    def start(t):
        i0, j0 = place(t)
        return pl.multiple_of(i0, TI), pl.multiple_of(j0, TJ)

    def products(t, slot):
        i0, j0 = start(t)

        def piece(k):
            if k < 2:
                prod[slot, k] = dot(left[pl.ds(i0, TI), :], right[k, :, pl.ds(j0, TJ)])
            else:
                prod[slot, k] = dot(left[pl.ds(i0, TI), 0:128], rightn[k - 2, :, pl.ds(j0, TJ)])

        return [functools.partial(piece, k) for k in range(4)]

    def values(t, slot):
        i0, j0 = start(t)

        def piece(jj, ii):
            lanes = pl.ds(j0 + jj * WIDE, WIDE)
            here = slice(jj * WIDE, (jj + 1) * WIDE)
            xj = [xj_ref[k : k + 1, lanes] for k in range(4)]
            rows = pl.ds(ii * SUB, SUB)
            halves = []
            for r in range(0, SUB, STEP):
                xi = [xi_ref[k, pl.ds(i0 + ii * SUB + r, STEP), :] for k in range(3)]
                xi = [jnp.concatenate([v, v], axis=1) for v in xi]
                pr = [prod[slot, k, pl.ds(ii * SUB + r, STEP), here] for k in range(4)]
                halves.append(pair_chunk(pr, xi, xj[0:3], xj[3]))
            a, b, c = [jnp.concatenate(parts, axis=0) for parts in zip(*halves)]
            for k, val in ((0, a), (2, c)):
                hi = val.astype(BF16)
                abc[slot, k, rows, here] = hi
                abc[slot, k + 1, rows, here] = (val - hi.astype(F32)).astype(BF16)
            abc[slot, 4, rows, here] = b.astype(BF16)

        return [functools.partial(piece, jj, ii) for jj in range(TJ // WIDE) for ii in range(TI // SUB)]

    def sums(t, slot):
        i0, j0 = start(t)
        kept = [None, None]
        groups = ((0, (0,)), (0, (1,)), (2, (2,)), (2, (3,)), (1, (4,)))

        def piece(n, k, parts):
            fi = frow[k, :, pl.ds(i0, TI)]
            add = dot(
                jnp.concatenate([fi] * len(parts), axis=1),
                jnp.concatenate([abc[slot, p] for p in parts], axis=0),
            )
            kept[0] = add if n == 0 else kept[0] + add
            if n == len(groups) - 1:
                ssum[:, pl.ds(j0, TJ)] += kept[0]

        def other(n, k, parts):
            fj = fcol[k, :, pl.ds(j0, TJ)]
            add = dot(
                jnp.concatenate([fj] * len(parts), axis=1),
                jnp.concatenate([abc[slot, p] for p in parts], axis=1),
                NT,
            )
            kept[1] = add if n == 0 else kept[1] + add
            if n == len(groups) - 1:
                tsum[:, pl.ds(i0, TI)] += kept[1]

        return [functools.partial(f, n, *g) for n, g in enumerate(groups) for f in (piece, other)]

    def interleave(vector, matrix):
        done = 0
        for n, todo in enumerate(vector):
            while done < len(matrix) and done * len(vector) <= n * len(matrix):
                matrix[done]()
                done += 1
            todo()

    last = count - 1
    for todo in products(0, 0):
        todo()
    abc[1] = jnp.zeros_like(abc[1])

    def double(u, _):
        t = 2 * u
        def half(h, _):
            @pl.when(h == 0)
            def _():
                interleave(values(t, 0), products(t + 1, 1) + sums(jnp.maximum(t - 1, 0), 1))

            @pl.when(h == 1)
            def _():
                interleave(values(t + 1, 1), products(jnp.minimum(t + 2, last), 0) + sums(t, 0))

            return 0

        lax.fori_loop(0, 2, half, 0)
        return 0

    lax.fori_loop(0, count // 2, double, 0)
    for todo in sums(last, 1):
        todo()


def pack_kernel(geo, adj, fwd, own, wt, tpack, spack, geo_v, own_v, wt_v, sems):
    copies = [
        pltpu.make_async_copy(src, dst, sems.at[k])
        for k, (src, dst) in enumerate(
            ((adj, tpack.at[0:64]), (fwd, spack.at[0:64]), (geo, geo_v), (own, own_v), (wt, wt_v))
        )
    ]
    for c in copies:
        c.start()
    for c in copies[2:]:
        c.wait()
    geo_rows = jnp.concatenate([geo_v[...], jnp.zeros_like(geo_v[0:1])], axis=0)
    own_rows = jnp.concatenate([wt_v[...], own_v[...].astype(F32)], axis=0)
    for pack in (tpack, spack):
        pack[64:72] = geo_rows
        pack[72:80] = own_rows
    for c in copies[:2]:
        c.wait()


def tile_place(n_j):
    return lambda t: ((t // n_j) * TI, lax.rem(t, n_j) * TJ)


def own_kernel(
    geo_ref, adj, fwd, near,
    right, rightn, xj_ref, fcol, tsum, ssum,
    left, xi_ref, frow, prod, abc,
):
    width = geo_ref.shape[1]
    geo = geo_ref[...]
    center = center_of(geo)
    first, second = pl.ds(0, width), pl.ds(width, width)
    build_targets(geo, adj[...], center, first, left, xi_ref, frow)
    build_sources(geo, fwd[...], center, first, right, rightn, xj_ref, fcol)
    build_sources(near[64:71], near[0:64], center, second, right, rightn, xj_ref, fcol)
    tsum[...] = jnp.zeros_like(tsum)
    ssum[...] = jnp.zeros_like(ssum)
    n_j = 2 * width // TJ
    run_tiles(
        (width // TI) * n_j, tile_place(n_j),
        left, right, rightn, xi_ref, xj_ref, frow, fcol, prod, abc, tsum, ssum,
    )


def reverse_bits(x, bits):
    out = jnp.zeros_like(x)
    for b in range(bits):
        out = out | (((x >> b) & 1) << (bits - 1 - b))
    return out


def rest_kernel(
    tpack, far, near, right, rightn, xj_ref, fcol, tsum_o, ssum_o,
    out_ref,
    left, xi_ref, frow, prod, abc, tsum, ssum,
):
    width = tpack.shape[1]
    geo, geo_s = tpack[64:71], near[64:71]
    center = center_of(geo)
    first, second = pl.ds(0, width), pl.ds(width, width)
    tsum[...] = jnp.zeros_like(tsum)
    ssum[...] = ssum_o[...]
    build_targets(far[64:71], far[0:64], center, first, left, xi_ref, frow)
    n_j = 2 * width // TJ
    run_tiles(
        (width // TI) * n_j, tile_place(n_j),
        left, right, rightn, xi_ref, xj_ref, frow, fcol, prod, abc, tsum, ssum,
    )

    def target_grad(g, acc):
        x = (g[0:3] - center) * TURNS
        m = g[3:6] * (1.0 / WAVENUM)
        sb, an, sc = read_sums(acc)
        gx = (2.0 * math.pi) * (x * sc[3:4] - sc[0:3]) + an - m * sb[3:4]
        gn = sb[0:3] - x * sb[3:4]
        return gx * TURNS, gn * (1.0 / WAVENUM)

    def source_grad(g, cols):
        x = (g[0:3] - center) * TURNS
        n = g[3:6]
        sa, bm, sc = read_sums(ssum[:, cols])
        gx = (2.0 * math.pi) * (x * sc[3:4] - sc[0:3]) - n * sa[3:4] + bm
        gn = sa[0:3] - x * sa[3:4]
        return gx * TURNS, gn

    t_own, s_own = target_grad(geo, tsum_o[...]), source_grad(geo, first)
    zero2 = jnp.zeros((2, width), F32)
    grads = [
        (t_own[0] + s_own[0], t_own[1] + s_own[1]),
        target_grad(far[64:71], tsum[...]),
        source_grad(geo_s, second),
    ]
    slots, _, cp_dev = out_ref.shape
    low_iota = lax.broadcasted_iota(jnp.int32, (2 * cp_dev, width), 0)
    terms = []
    for (gx, gn), rows in zip(grads, (tpack[72:80], far[72:80], near[72:80])):
        own_of, wt_of = rows[4:8].astype(jnp.int32), rows[0:4]
        g = jnp.concatenate([gx, gn, zero2], axis=0)
        place_of = reverse_bits(own_of // cp_dev, slots.bit_length() - 1)
        low = lax.rem(own_of, cp_dev) + (place_of & 1) * cp_dev
        place_of = place_of >> 1
        for s in range(4):
            gw = g * wt_of[s : s + 1]
            hi = hi_part(gw)
            here = jnp.where(low[s : s + 1] == low_iota, 1.0, 0.0).astype(BF16)
            both = jnp.concatenate([hi, gw - hi], axis=0).astype(BF16)
            where_to = jnp.broadcast_to(place_of[s : s + 1].astype(F32), both.shape).astype(BF16)
            terms.append((where_to, both, here))
    onehot = jnp.concatenate([t[2] for t in terms], axis=1)
    where_to = jnp.concatenate([t[0] for t in terms], axis=1)
    both = jnp.concatenate([t[1] for t in terms], axis=1)

    def add_owner(s0):
        rows = [jnp.where(where_to == (s0 // 2 + r), both, jnp.zeros_like(both)) for r in range(8)]
        acc = dot(jnp.concatenate(rows, axis=0), onehot, NT).reshape(8, 16, 2 * cp_dev)
        acc = acc[:, 0:8] + acc[:, 8:16]
        for r in range(8):
            out_ref[s0 + 2 * r] = acc[r, :, 0:cp_dev]
            out_ref[s0 + 2 * r + 1] = acc[r, :, cp_dev:]

    for s0 in range(0, slots, 16):
        add_owner(s0)


def shape(dims, kind):
    return jax.ShapeDtypeStruct(dims, kind)


def tile_scratch():
    return [pltpu.VMEM((2, 4, TI, TJ), F32), pltpu.VMEM((2, 5, TI, TJ), BF16)]


PARAMS = pltpu.CompilerParams(vmem_limit_bytes=20 * 1024 * 1024)


def pack_call(geo, adj, fwd, own, wt):
    width = geo.shape[1]
    return pl.pallas_call(
        pack_kernel,
        in_specs=[pl.BlockSpec(memory_space=pl.ANY)] * 5,
        out_shape=[shape((80, width), F32)] * 2,
        scratch_shapes=[
            pltpu.VMEM((7, width), F32), pltpu.VMEM((4, width), jnp.int32), pltpu.VMEM((4, width), F32),
            pltpu.SemaphoreType.DMA((5,)),
        ],
        name="pack",
    )(geo, adj, fwd, own, wt)


def target_scratch(width):
    return [
        pltpu.VMEM((width, 256), BF16), pltpu.VMEM((3, width, LANE), F32), pltpu.VMEM((3, 32, width), BF16)
    ] + tile_scratch()


def own_call(args):
    width = args[0].shape[1]
    total = 2 * width
    return pl.pallas_call(
        own_kernel,
        out_shape=[
            shape((2, 256, total), BF16), shape((2, 128, total), BF16), shape((8, total), F32),
            shape((3, 32, total), BF16), shape((32, width), F32), shape((32, total), F32),
        ],
        scratch_shapes=target_scratch(width),
        compiler_params=PARAMS,
        cost_estimate=pl.CostEstimate(flops=8 * 10**9, bytes_accessed=4 * 10**6, transcendentals=0),
        name="own",
    )(*args)


def rest_call(args, slots, cp_dev):
    width = args[0].shape[1]
    return pl.pallas_call(
        rest_kernel,
        out_shape=shape((slots, 8, cp_dev), F32),
        scratch_shapes=target_scratch(width) + [pltpu.VMEM((32, width), F32), pltpu.VMEM((32, 2 * width), F32)],
        compiler_params=PARAMS,
        cost_estimate=pl.CostEstimate(flops=8 * 10**9, bytes_accessed=4 * 10**6, transcendentals=0),
        name="rest",
    )(*args)


def swap(x, axis, bit):
    size = lax.axis_size(axis)
    return lax.ppermute(x, axis, [(k, k ^ bit) for k in range(size)])


def halving(cur):
    n_loop = lax.axis_size("loop").bit_length() - 1
    n_row = lax.axis_size("row").bit_length() - 1
    steps = [("loop", 1 << b) for b in range(n_loop)] + [("row", 1 << b) for b in range(n_row)]
    for axis, bit in steps:
        half = cur.shape[0] // 2
        up = jnp.where((lax.axis_index(axis) & bit) > 0, 1, 0)
        keep = lax.dynamic_slice_in_dim(cur, up * half, half, 0)
        send = lax.dynamic_slice_in_dim(cur, (1 - up) * half, half, 0)
        cur = keep + swap(send, axis, bit)
    return cur[0, 0:6]


def on_device(cp_dev, geometry, adjoint, forward, owner_map, owner_weight):
    slots = lax.axis_size("row") * lax.axis_size("loop")
    tpack, spack = pack_call(geometry, adjoint, forward, owner_map, owner_weight)
    near = swap(spack, "loop", 1)
    far = swap(tpack, "loop", 2)
    tables = own_call((geometry, adjoint, forward, near))
    return halving(rest_call((tpack, far, near, *tables), slots, cp_dev))


def solution(mesh):
    spec = P(None, ("parts", "row", "loop"))
    return jax.shard_map(
        functools.partial(on_device, 32), mesh=mesh, in_specs=(spec,) * 5, out_specs=spec, check_vma=False
    )
```

```python
import functools
import math

import jax
import jax.numpy as jnp
from jax import lax
from jax.experimental import pallas as pl
from jax.experimental.pallas import tpu as pltpu
from jax.sharding import PartitionSpec as P

WAVENUM = 2.0 * math.pi * 6000.0 / 1500.0
TURNS = WAVENUM / (2.0 * math.pi)
PAIR_SCALE = WAVENUM**3 / (4.0 * math.pi * TURNS)
F32 = jnp.float32
BF16 = jnp.bfloat16
TI = 256
TJ = 256
SUB = 16
STEP = 8
LANE = 128
WIDE = 256


def _fit(fn, odd, terms):
    import numpy as np

    nodes = 0.5 * np.cos(np.pi * (np.arange(400) + 0.5) / 400)
    cols = np.stack([nodes ** (2 * n + odd) for n in range(terms)], axis=1)
    coef = np.linalg.lstsq(cols, fn(nodes), rcond=None)[0]
    return [float(np.float32(c)) for c in coef]


def _sine():
    import numpy as np

    return _fit(lambda t: math.sqrt(2.0) * np.sin(np.pi * t), 1, 5)


SIN_C = _sine()


def horner(coef, y):
    acc = coef[-1] * y + coef[-2]
    for c in coef[-3::-1]:
        acc = acc * y + c
    return acc


def hi_part(x):
    return x.astype(BF16).astype(F32)


def split3(x):
    one = hi_part(x)
    rest = x - one
    two = hi_part(rest)
    return one, two, rest - two


SPLIT_PAIRS = ((0, 0), (0, 1), (1, 0), (0, 2), (2, 0), (1, 1), (1, 2), (2, 1))


def rows8(x, n, a, b):
    return jnp.concatenate([x, n, a, b], axis=0)


def target_rows(geo, center):
    x = (geo[0:3] - center) * TURNS
    m = geo[3:6] * (1.0 / WAVENUM)
    ones = jnp.ones_like(x[0:1])
    xm = jnp.sum(x * m, axis=0, keepdims=True)
    return x, m, split3(rows8(x, m, ones, xm))


def target_table(adj, rows):
    hi = hi_part(adj)
    lo = adj - hi
    return jnp.concatenate([rows[a] for a, _ in SPLIT_PAIRS] + [hi, hi, lo], axis=0)


def source_rows(geo, center):
    x = (geo[0:3] - center) * TURNS
    n = geo[3:6]
    return x, n


def source_table(geo, fwd, x, n):
    area = geo[6:7]
    scaled = fwd * (area * PAIR_SCALE)
    re, im = scaled[0:32], scaled[32:64]
    real = jnp.concatenate([re, im], axis=0)
    imag = jnp.concatenate([im, -re], axis=0)
    rh, ih = hi_part(real), hi_part(imag)
    zero3 = jnp.zeros_like(x)
    zero1 = jnp.zeros_like(x[0:1])
    ones = jnp.ones_like(zero1)
    xn = jnp.sum(x * n, axis=0, keepdims=True)
    prow = split3(rows8(-n, zero3, xn, zero1))
    qrow = split3(rows8(zero3, -x, zero1, ones))
    zeros = jnp.zeros((64, x.shape[1]), F32)
    cols = [
        jnp.concatenate([zeros, rh, real - rh, rh], axis=0),
        jnp.concatenate([zeros, ih, imag - ih, ih], axis=0),
        jnp.concatenate([prow[b] for _, b in SPLIT_PAIRS] + [zeros], axis=0),
        jnp.concatenate([qrow[b] for _, b in SPLIT_PAIRS] + [zeros], axis=0),
    ]
    return cols


def pair_chunk(prod, xi, xj, area):
    wr, wi, pn, q = prod
    d0, d1, d2 = xi[0] - xj[0], xi[1] - xj[1], xi[2] - xj[2]
    r2 = (d0 * d0 + d1 * d1) + (d2 * d2 + area)
    rs = lax.rsqrt(r2)
    turns = r2 * rs
    t = turns - jnp.round(turns)
    v = rs * (1.0 / (2.0 * math.pi))
    y = t * t
    sv = (t * v) * horner(SIN_C, y)
    v2 = v * v
    ec = v2 - sv * sv
    cv2 = jnp.maximum(v2 + ec, 1e-30)
    es = (sv * cv2) * lax.rsqrt(cv2)
    yr = ec * wr - es * wi
    yi = ec * wi + es * wr
    a = yi + v * yr
    b = yr - v * yi
    c = rs * ((q * yi - pn * yr) + (3.0 * v) * (pn * a + q * b))
    return a, b, c


def dot(a, b, dims=(((1,), (0,)), ((), ()))):
    return lax.dot_general(a, b, dims, preferred_element_type=F32)


def sum_splits(x):
    return x[0:8] + x[8:16] + x[16:24]


NT = (((1,), (1,)), ((), ()))


def sum_rows(x, n):
    width = x.shape[1]
    zero = jnp.zeros((1, width), F32)
    x1, x2, x3 = split3(x)
    n1 = hi_part(n)
    xr = jnp.concatenate([x1, jnp.ones_like(zero), x2, zero, x3, zero], axis=0)
    nr = jnp.concatenate([n1, zero, n - n1, zero], axis=0)
    z12, z20 = jnp.zeros((12, width), F32), jnp.zeros((20, width), F32)
    rows = ([xr, z20], [z12, nr, z12], [z20, xr])
    return [jnp.concatenate(r, axis=0).astype(BF16) for r in rows]


def read_sums(acc):
    return acc[0:4] + acc[4:8] + acc[8:12], acc[12:15] + acc[16:19], acc[20:24] + acc[24:28] + acc[28:32]


def build_targets(geo, adj, center, cols, left, xi_ref, frow):
    x, m, rows = target_rows(geo, center)
    left[cols, :] = target_table(adj, rows).T.astype(BF16)
    sums = sum_rows(x, m)
    for k in range(3):
        frow[k, :, cols] = sums[k]
    row = lax.broadcasted_iota(jnp.int32, (128, 3 * LANE), 0)
    axis = lax.broadcasted_iota(jnp.int32, (128, 3 * LANE), 1) // LANE
    pick = (row == axis) | (row == axis + 16) | (row == axis + 32)
    spread = dot(left[cols, 0:128], jnp.where(pick, 1.0, 0.0).astype(BF16))
    for k in range(3):
        xi_ref[k, cols, :] = spread[:, k * LANE : (k + 1) * LANE]


def build_sources(geo, fwd, center, cols, right, rightn, xj_ref, fcol):
    x, n = source_rows(geo, center)
    xj_ref[:, cols] = jnp.concatenate([x, geo[6:7] * (TURNS * TURNS)] * 2, axis=0)
    tab = source_table(geo, fwd, x, n)
    for k in range(2):
        right[k, :, cols] = tab[k].astype(BF16)
        rightn[k, :, cols] = tab[k + 2].astype(BF16)
    sums = sum_rows(x, n)
    for k, part in enumerate((sums[1], sums[0], sums[2])):
        fcol[k, :, cols] = part


def center_of(geo):
    return jnp.round(jnp.mean(geo[0:3], axis=1, keepdims=True))


def run_tiles(count, place, left, right, rightn, xi_ref, xj_ref, frow, fcol, prod, abc, tsum, ssum):
    def start(t):
        i0, j0 = place(t)
        return pl.multiple_of(i0, TI), pl.multiple_of(j0, TJ)

    def products(t, slot):
        i0, j0 = start(t)

        def piece(k):
            if k < 2:
                prod[slot, k] = dot(left[pl.ds(i0, TI), :], right[k, :, pl.ds(j0, TJ)])
            else:
                prod[slot, k] = dot(left[pl.ds(i0, TI), 0:128], rightn[k - 2, :, pl.ds(j0, TJ)])

        return [functools.partial(piece, k) for k in range(4)]

    def values(t, slot):
        i0, j0 = start(t)

        def piece(jj, ii):
            lanes = pl.ds(j0 + jj * WIDE, WIDE)
            here = slice(jj * WIDE, (jj + 1) * WIDE)
            xj = [xj_ref[k : k + 1, lanes] for k in range(4)]
            rows = pl.ds(ii * SUB, SUB)
            halves = []
            for r in range(0, SUB, STEP):
                xi = [xi_ref[k, pl.ds(i0 + ii * SUB + r, STEP), :] for k in range(3)]
                xi = [jnp.concatenate([v, v], axis=1) for v in xi]
                pr = [prod[slot, k, pl.ds(ii * SUB + r, STEP), here] for k in range(4)]
                halves.append(pair_chunk(pr, xi, xj[0:3], xj[3]))
            a, b, c = [jnp.concatenate(parts, axis=0) for parts in zip(*halves)]
            for k, val in ((0, a), (2, c)):
                hi = val.astype(BF16)
                abc[slot, k, rows, here] = hi
                abc[slot, k + 1, rows, here] = (val - hi.astype(F32)).astype(BF16)
            abc[slot, 4, rows, here] = b.astype(BF16)

        return [functools.partial(piece, jj, ii) for jj in range(TJ // WIDE) for ii in range(TI // SUB)]

    def sums(t, slot):
        i0, j0 = start(t)
        kept = [None, None]
        groups = ((0, (0,)), (0, (1,)), (2, (2,)), (2, (3,)), (1, (4,)))

        def piece(n, k, parts):
            fi = frow[k, :, pl.ds(i0, TI)]
            add = dot(
                jnp.concatenate([fi] * len(parts), axis=1),
                jnp.concatenate([abc[slot, p] for p in parts], axis=0),
            )
            kept[0] = add if n == 0 else kept[0] + add
            if n == len(groups) - 1:
                ssum[:, pl.ds(j0, TJ)] += kept[0]

        def other(n, k, parts):
            fj = fcol[k, :, pl.ds(j0, TJ)]
            add = dot(
                jnp.concatenate([fj] * len(parts), axis=1),
                jnp.concatenate([abc[slot, p] for p in parts], axis=1),
                NT,
            )
            kept[1] = add if n == 0 else kept[1] + add
            if n == len(groups) - 1:
                tsum[:, pl.ds(i0, TI)] += kept[1]

        return [functools.partial(f, n, *g) for n, g in enumerate(groups) for f in (piece, other)]

    def interleave(vector, matrix):
        done = 0
        for n, todo in enumerate(vector):
            while done < len(matrix) and done * len(vector) <= n * len(matrix):
                matrix[done]()
                done += 1
            todo()

    last = count - 1
    for todo in products(0, 0):
        todo()
    abc[1] = jnp.zeros_like(abc[1])

    def double(u, _):
        t = 2 * u
        def half(h, _):
            @pl.when(h == 0)
            def _():
                interleave(values(t, 0), products(t + 1, 1) + sums(jnp.maximum(t - 1, 0), 1))

            @pl.when(h == 1)
            def _():
                interleave(values(t + 1, 1), products(jnp.minimum(t + 2, last), 0) + sums(t, 0))

            return 0

        lax.fori_loop(0, 2, half, 0)
        return 0

    lax.fori_loop(0, count // 2, double, 0)
    for todo in sums(last, 1):
        todo()


def pack_kernel(geo, adj, fwd, own, wt, tpack, spack, geo_v, own_v, wt_v, sems):
    copies = [
        pltpu.make_async_copy(src, dst, sems.at[k])
        for k, (src, dst) in enumerate(
            ((adj, tpack.at[0:64]), (fwd, spack.at[0:64]), (geo, geo_v), (own, own_v), (wt, wt_v))
        )
    ]
    for c in copies:
        c.start()
    for c in copies[2:]:
        c.wait()
    geo_rows = jnp.concatenate([geo_v[...], jnp.zeros_like(geo_v[0:1])], axis=0)
    own_rows = jnp.concatenate([wt_v[...], own_v[...].astype(F32)], axis=0)
    for pack in (tpack, spack):
        pack[64:72] = geo_rows
        pack[72:80] = own_rows
    for c in copies[:2]:
        c.wait()


def tile_place(n_j):
    return lambda t: ((t // n_j) * TI, lax.rem(t, n_j) * TJ)


def own_kernel(
    geo_ref, adj, fwd, near,
    right, rightn, xj_ref, fcol, tsum, ssum,
    left, xi_ref, frow, prod, abc,
):
    width = geo_ref.shape[1]
    geo = geo_ref[...]
    center = center_of(geo)
    first, second = pl.ds(0, width), pl.ds(width, width)
    build_targets(geo, adj[...], center, first, left, xi_ref, frow)
    build_sources(geo, fwd[...], center, first, right, rightn, xj_ref, fcol)
    build_sources(near[64:71], near[0:64], center, second, right, rightn, xj_ref, fcol)
    tsum[...] = jnp.zeros_like(tsum)
    ssum[...] = jnp.zeros_like(ssum)
    n_j = 2 * width // TJ
    run_tiles(
        (width // TI) * n_j, tile_place(n_j),
        left, right, rightn, xi_ref, xj_ref, frow, fcol, prod, abc, tsum, ssum,
    )


def reverse_bits(x, bits):
    out = jnp.zeros_like(x)
    for b in range(bits):
        out = out | (((x >> b) & 1) << (bits - 1 - b))
    return out


def rest_kernel(
    tpack, far, near, right, rightn, xj_ref, fcol, tsum_o, ssum_o,
    out_ref,
    left, xi_ref, frow, prod, abc, tsum, ssum,
):
    width = tpack.shape[1]
    geo, geo_s = tpack[64:71], near[64:71]
    center = center_of(geo)
    first, second = pl.ds(0, width), pl.ds(width, width)
    tsum[...] = jnp.zeros_like(tsum)
    ssum[...] = ssum_o[...]
    build_targets(far[64:71], far[0:64], center, first, left, xi_ref, frow)
    n_j = 2 * width // TJ
    run_tiles(
        (width // TI) * n_j, tile_place(n_j),
        left, right, rightn, xi_ref, xj_ref, frow, fcol, prod, abc, tsum, ssum,
    )

    def target_grad(g, acc):
        x = (g[0:3] - center) * TURNS
        m = g[3:6] * (1.0 / WAVENUM)
        sb, an, sc = read_sums(acc)
        gx = (2.0 * math.pi) * (x * sc[3:4] - sc[0:3]) + an - m * sb[3:4]
        gn = sb[0:3] - x * sb[3:4]
        return gx * TURNS, gn * (1.0 / WAVENUM)

    def source_grad(g, cols):
        x = (g[0:3] - center) * TURNS
        n = g[3:6]
        sa, bm, sc = read_sums(ssum[:, cols])
        gx = (2.0 * math.pi) * (x * sc[3:4] - sc[0:3]) - n * sa[3:4] + bm
        gn = sa[0:3] - x * sa[3:4]
        return gx * TURNS, gn

    t_own, s_own = target_grad(geo, tsum_o[...]), source_grad(geo, first)
    zero2 = jnp.zeros((2, width), F32)
    grads = [
        (t_own[0] + s_own[0], t_own[1] + s_own[1]),
        target_grad(far[64:71], tsum[...]),
        source_grad(geo_s, second),
    ]
    slots, _, cp_dev = out_ref.shape
    low_iota = lax.broadcasted_iota(jnp.int32, (2 * cp_dev, width), 0)
    terms = []
    for (gx, gn), rows in zip(grads, (tpack[72:80], far[72:80], near[72:80])):
        own_of, wt_of = rows[4:8].astype(jnp.int32), rows[0:4]
        g = jnp.concatenate([gx, gn, zero2], axis=0)
        place_of = reverse_bits(own_of // cp_dev, slots.bit_length() - 1)
        low = lax.rem(own_of, cp_dev) + (place_of & 1) * cp_dev
        place_of = place_of >> 1
        for s in range(4):
            gw = g * wt_of[s : s + 1]
            hi = hi_part(gw)
            here = jnp.where(low[s : s + 1] == low_iota, 1.0, 0.0).astype(BF16)
            both = jnp.concatenate([hi, gw - hi], axis=0).astype(BF16)
            where_to = jnp.broadcast_to(place_of[s : s + 1].astype(F32), both.shape).astype(BF16)
            terms.append((where_to, both, here))
    onehot = jnp.concatenate([t[2] for t in terms], axis=1)
    where_to = jnp.concatenate([t[0] for t in terms], axis=1)
    both = jnp.concatenate([t[1] for t in terms], axis=1)

    def add_owner(s0):
        rows = [jnp.where(where_to == (s0 // 2 + r), both, jnp.zeros_like(both)) for r in range(8)]
        acc = dot(jnp.concatenate(rows, axis=0), onehot, NT).reshape(8, 16, 2 * cp_dev)
        acc = acc[:, 0:8] + acc[:, 8:16]
        for r in range(8):
            out_ref[s0 + 2 * r] = acc[r, :, 0:cp_dev]
            out_ref[s0 + 2 * r + 1] = acc[r, :, cp_dev:]

    for s0 in range(0, slots, 16):
        add_owner(s0)


def shape(dims, kind):
    return jax.ShapeDtypeStruct(dims, kind)


def tile_scratch():
    return [pltpu.VMEM((2, 4, TI, TJ), F32), pltpu.VMEM((2, 5, TI, TJ), BF16)]


PARAMS = pltpu.CompilerParams(vmem_limit_bytes=20 * 1024 * 1024)


def pack_call(geo, adj, fwd, own, wt):
    width = geo.shape[1]
    return pl.pallas_call(
        pack_kernel,
        in_specs=[pl.BlockSpec(memory_space=pl.ANY)] * 5,
        out_shape=[shape((80, width), F32)] * 2,
        scratch_shapes=[
            pltpu.VMEM((7, width), F32), pltpu.VMEM((4, width), jnp.int32), pltpu.VMEM((4, width), F32),
            pltpu.SemaphoreType.DMA((5,)),
        ],
        name="pack",
    )(geo, adj, fwd, own, wt)


def target_scratch(width):
    return [
        pltpu.VMEM((width, 256), BF16), pltpu.VMEM((3, width, LANE), F32), pltpu.VMEM((3, 32, width), BF16)
    ] + tile_scratch()


def own_call(args):
    width = args[0].shape[1]
    total = 2 * width
    return pl.pallas_call(
        own_kernel,
        out_shape=[
            shape((2, 256, total), BF16), shape((2, 128, total), BF16), shape((8, total), F32),
            shape((3, 32, total), BF16), shape((32, width), F32), shape((32, total), F32),
        ],
        scratch_shapes=target_scratch(width),
        compiler_params=PARAMS,
        cost_estimate=pl.CostEstimate(flops=8 * 10**9, bytes_accessed=4 * 10**6, transcendentals=0),
        name="own",
    )(*args)


def rest_call(args, slots, cp_dev):
    width = args[0].shape[1]
    return pl.pallas_call(
        rest_kernel,
        out_shape=shape((slots, 8, cp_dev), F32),
        scratch_shapes=target_scratch(width) + [pltpu.VMEM((32, width), F32), pltpu.VMEM((32, 2 * width), F32)],
        compiler_params=PARAMS,
        cost_estimate=pl.CostEstimate(flops=8 * 10**9, bytes_accessed=4 * 10**6, transcendentals=0),
        name="rest",
    )(*args)


def swap(x, axis, bit):
    size = lax.axis_size(axis)
    return lax.ppermute(x, axis, [(k, k ^ bit) for k in range(size)])


def halving(cur):
    n_loop = lax.axis_size("loop").bit_length() - 1
    n_row = lax.axis_size("row").bit_length() - 1
    steps = [("loop", 1 << b) for b in range(n_loop)] + [("row", 1 << b) for b in range(n_row)]
    for axis, bit in steps:
        half = cur.shape[0] // 2
        up = jnp.where((lax.axis_index(axis) & bit) > 0, 1, 0)
        keep = lax.dynamic_slice_in_dim(cur, up * half, half, 0)
        send = lax.dynamic_slice_in_dim(cur, (1 - up) * half, half, 0)
        cur = keep + swap(send, axis, bit)
    return cur[0, 0:6]


def on_device(cp_dev, geometry, adjoint, forward, owner_map, owner_weight):
    slots = lax.axis_size("row") * lax.axis_size("loop")
    tpack, spack = pack_call(geometry, adjoint, forward, owner_map, owner_weight)
    near = swap(spack, "loop", 1)
    far = swap(tpack, "loop", 2)
    tables = own_call((geometry, adjoint, forward, near))
    return halving(rest_call((tpack, far, near, *tables), slots, cp_dev))


def solution(mesh):
    spec = P(None, ("parts", "row", "loop"))
    return jax.shard_map(
        functools.partial(on_device, 32), mesh=mesh, in_specs=(spec,) * 5, out_specs=spec, check_vma=False
    )
```

```python
import functools
import math

import jax
import jax.numpy as jnp
from jax import lax
from jax.experimental import pallas as pl
from jax.experimental.pallas import tpu as pltpu
from jax.sharding import PartitionSpec as P

WAVENUM = 2.0 * math.pi * 6000.0 / 1500.0
TURNS = WAVENUM / (2.0 * math.pi)
PAIR_SCALE = WAVENUM**3 / (4.0 * math.pi * TURNS)
F32 = jnp.float32
BF16 = jnp.bfloat16
TI = 256
TJ = 256
SUB = 16
STEP = 8
LAST = 32
LAST_STEP = 16
LANE = 128
WIDE = 256


def _fit(fn, odd, terms):
    import numpy as np

    nodes = 0.5 * np.cos(np.pi * (np.arange(400) + 0.5) / 400)
    cols = np.stack([nodes ** (2 * n + odd) for n in range(terms)], axis=1)
    coef = np.linalg.lstsq(cols, fn(nodes), rcond=None)[0]
    return [float(np.float32(c)) for c in coef]


def _sine():
    import numpy as np

    return _fit(lambda t: math.sqrt(2.0) * np.sin(np.pi * t), 1, 5)


SIN_C = _sine()


def horner(coef, y):
    acc = coef[-1] * y + coef[-2]
    for c in coef[-3::-1]:
        acc = acc * y + c
    return acc


def hi_part(x):
    return x.astype(BF16).astype(F32)


def split3(x):
    one = hi_part(x)
    rest = x - one
    two = hi_part(rest)
    return one, two, rest - two


SPLIT_PAIRS = ((0, 0), (0, 1), (1, 0), (0, 2), (2, 0), (1, 1), (1, 2), (2, 1))


def rows8(x, n, a, b):
    return jnp.concatenate([x, n, a, b], axis=0)


def target_rows(geo, center):
    x = (geo[0:3] - center) * TURNS
    m = geo[3:6] * (1.0 / WAVENUM)
    ones = jnp.ones_like(x[0:1])
    xm = jnp.sum(x * m, axis=0, keepdims=True)
    return x, m, split3(rows8(x, m, ones, xm))


def target_table(adj, rows):
    hi = hi_part(adj)
    lo = adj - hi
    return jnp.concatenate([rows[a] for a, _ in SPLIT_PAIRS] + [hi, hi, lo], axis=0)


def source_rows(geo, center):
    x = (geo[0:3] - center) * TURNS
    n = geo[3:6]
    return x, n


def source_table(geo, fwd, x, n):
    area = geo[6:7]
    scaled = fwd * (area * PAIR_SCALE)
    re, im = scaled[0:32], scaled[32:64]
    real = jnp.concatenate([re, im], axis=0)
    imag = jnp.concatenate([im, -re], axis=0)
    rh, ih = hi_part(real), hi_part(imag)
    zero3 = jnp.zeros_like(x)
    zero1 = jnp.zeros_like(x[0:1])
    ones = jnp.ones_like(zero1)
    xn = jnp.sum(x * n, axis=0, keepdims=True)
    prow = split3(rows8(-n, zero3, xn, zero1))
    qrow = split3(rows8(zero3, -x, zero1, ones))
    zeros = jnp.zeros((64, x.shape[1]), F32)
    cols = [
        jnp.concatenate([zeros, rh, real - rh, rh], axis=0),
        jnp.concatenate([zeros, ih, imag - ih, ih], axis=0),
        jnp.concatenate([prow[b] for _, b in SPLIT_PAIRS] + [zeros], axis=0),
        jnp.concatenate([qrow[b] for _, b in SPLIT_PAIRS] + [zeros], axis=0),
    ]
    return cols


def pair_chunk(prod, xi, xj, area):
    wr, wi, pn, q = prod
    d0, d1, d2 = xi[0] - xj[0], xi[1] - xj[1], xi[2] - xj[2]
    r2 = (d0 * d0 + d1 * d1) + (d2 * d2 + area)
    rs = lax.rsqrt(r2)
    turns = r2 * rs
    t = turns - jnp.round(turns)
    v = rs * (1.0 / (2.0 * math.pi))
    y = t * t
    sv = (t * v) * horner(SIN_C, y)
    v2 = v * v
    ec = v2 - sv * sv
    cv2 = jnp.maximum(v2 + ec, 1e-30)
    es = (sv * cv2) * lax.rsqrt(cv2)
    yr = ec * wr - es * wi
    yi = ec * wi + es * wr
    a = yi + v * yr
    b = yr - v * yi
    c = rs * ((q * yi - pn * yr) + (3.0 * v) * (pn * a + q * b))
    return a, b, c


def dot(a, b, dims=(((1,), (0,)), ((), ()))):
    return lax.dot_general(a, b, dims, preferred_element_type=F32)


def sum_splits(x):
    return x[0:8] + x[8:16] + x[16:24]


NT = (((1,), (1,)), ((), ()))


def sum_rows(x, n):
    width = x.shape[1]
    zero = jnp.zeros((1, width), F32)
    x1, x2, x3 = split3(x)
    n1 = hi_part(n)
    xr = jnp.concatenate([x1, jnp.ones_like(zero), x2, zero, x3, zero], axis=0)
    nr = jnp.concatenate([n1, zero, n - n1, zero], axis=0)
    z12, z20 = jnp.zeros((12, width), F32), jnp.zeros((20, width), F32)
    rows = ([xr, z20], [z12, nr, z12], [z20, xr])
    return [jnp.concatenate(r, axis=0).astype(BF16) for r in rows]


def read_sums(acc):
    return acc[0:4] + acc[4:8] + acc[8:12], acc[12:15] + acc[16:19], acc[20:24] + acc[24:28] + acc[28:32]


def build_targets(geo, adj, center, cols, left, xi_ref, frow):
    x, m, rows = target_rows(geo, center)
    left[cols, :] = target_table(adj, rows).T.astype(BF16)
    sums = sum_rows(x, m)
    for k in range(3):
        frow[k, :, cols] = sums[k]
    row = lax.broadcasted_iota(jnp.int32, (128, 3 * LANE), 0)
    axis = lax.broadcasted_iota(jnp.int32, (128, 3 * LANE), 1) // LANE
    pick = (row == axis) | (row == axis + 16) | (row == axis + 32)
    spread = dot(left[cols, 0:128], jnp.where(pick, 1.0, 0.0).astype(BF16))
    for k in range(3):
        xi_ref[k, cols, :] = spread[:, k * LANE : (k + 1) * LANE]


def build_sources(geo, fwd, center, cols, right, rightn, xj_ref, fcol):
    x, n = source_rows(geo, center)
    xj_ref[:, cols] = jnp.concatenate([x, geo[6:7] * (TURNS * TURNS)] * 2, axis=0)
    tab = source_table(geo, fwd, x, n)
    for k in range(2):
        right[k, :, cols] = tab[k].astype(BF16)
        rightn[k, :, cols] = tab[k + 2].astype(BF16)
    sums = sum_rows(x, n)
    for k, part in enumerate((sums[1], sums[0], sums[2])):
        fcol[k, :, cols] = part


def center_of(geo):
    return jnp.round(jnp.mean(geo[0:3], axis=1, keepdims=True))


def run_tiles(count, place, left, right, rightn, xi_ref, xj_ref, frow, fcol, prod, abc, tsum, ssum):
    def start(t):
        i0, j0 = place(t)
        return pl.multiple_of(i0, TI), pl.multiple_of(j0, TJ)

    def products(t, slot):
        i0, j0 = start(t)

        def piece(k):
            if k < 2:
                prod[slot, k] = dot(left[pl.ds(i0, TI), :], right[k, :, pl.ds(j0, TJ)])
            else:
                prod[slot, k] = dot(left[pl.ds(i0, TI), 0:128], rightn[k - 2, :, pl.ds(j0, TJ)])

        return [functools.partial(piece, k) for k in range(4)]

    def values(t, slot):
        i0, j0 = start(t)

        def piece(jj, top, size, step):
            here = slice(jj * WIDE, (jj + 1) * WIDE)
            xj = [xj_ref[k : k + 1, pl.ds(j0 + jj * WIDE, WIDE)] for k in range(4)]
            rows = pl.ds(top, size)
            bands = []
            for r in range(top, top + size, step):
                xi = [xi_ref[k, pl.ds(i0 + r, step), :] for k in range(3)]
                xi = [jnp.concatenate([v, v], axis=1) for v in xi]
                pr = [prod[slot, k, pl.ds(r, step), here] for k in range(4)]
                bands.append(pair_chunk(pr, xi, xj[0:3], xj[3]))
            a, b, c = [jnp.concatenate(parts, axis=0) for parts in zip(*bands)]
            for k, val in ((0, a), (2, c)):
                hi = val.astype(BF16)
                abc[slot, k, rows, here] = hi
                abc[slot, k + 1, rows, here] = (val - hi.astype(F32)).astype(BF16)
            abc[slot, 4, rows, here] = b.astype(BF16)

        todo = [(jj, top, SUB, STEP) for jj in range(TJ // WIDE) for top in range(0, TI, SUB)]
        if LAST > SUB:
            todo = todo[: -(LAST // SUB)] + [(TJ // WIDE - 1, TI - LAST, LAST, LAST_STEP)]
        return [functools.partial(piece, *args) for args in todo]

    def sums(t, slot):
        i0, j0 = start(t)
        kept = [None, None]
        groups = ((0, (0,)), (0, (1,)), (2, (2,)), (2, (3,)), (1, (4,)))

        def piece(n, k, parts):
            fi = frow[k, :, pl.ds(i0, TI)]
            add = dot(
                jnp.concatenate([fi] * len(parts), axis=1),
                jnp.concatenate([abc[slot, p] for p in parts], axis=0),
            )
            kept[0] = add if n == 0 else kept[0] + add
            if n == len(groups) - 1:
                ssum[:, pl.ds(j0, TJ)] += kept[0]

        def other(n, k, parts):
            fj = fcol[k, :, pl.ds(j0, TJ)]
            add = dot(
                jnp.concatenate([fj] * len(parts), axis=1),
                jnp.concatenate([abc[slot, p] for p in parts], axis=1),
                NT,
            )
            kept[1] = add if n == 0 else kept[1] + add
            if n == len(groups) - 1:
                tsum[:, pl.ds(i0, TI)] += kept[1]

        return [functools.partial(f, n, *g) for n, g in enumerate(groups) for f in (piece, other)]

    def interleave(vector, matrix):
        done = 0
        for n, todo in enumerate(vector):
            while done < len(matrix) and done * len(vector) <= n * len(matrix):
                matrix[done]()
                done += 1
            todo()
        for rest in matrix[done:]:
            rest()

    last = count - 1
    for todo in products(0, 0):
        todo()
    abc[1] = jnp.zeros_like(abc[1])

    def double(u, _):
        t = 2 * u
        def half(h, _):
            @pl.when(h == 0)
            def _():
                interleave(values(t, 0), products(t + 1, 1) + sums(jnp.maximum(t - 1, 0), 1))

            @pl.when(h == 1)
            def _():
                interleave(values(t + 1, 1), products(jnp.minimum(t + 2, last), 0) + sums(t, 0))

            return 0

        lax.fori_loop(0, 2, half, 0)
        return 0

    lax.fori_loop(0, count // 2, double, 0)
    for todo in sums(last, 1):
        todo()


def pack_kernel(geo, adj, fwd, own, wt, tpack, spack, geo_v, own_v, wt_v, sems):
    copies = [
        pltpu.make_async_copy(src, dst, sems.at[k])
        for k, (src, dst) in enumerate(
            ((adj, tpack.at[0:64]), (fwd, spack.at[0:64]), (geo, geo_v), (own, own_v), (wt, wt_v))
        )
    ]
    for c in copies:
        c.start()
    for c in copies[2:]:
        c.wait()
    geo_rows = jnp.concatenate([geo_v[...], jnp.zeros_like(geo_v[0:1])], axis=0)
    own_rows = jnp.concatenate([wt_v[...], own_v[...].astype(F32)], axis=0)
    for pack in (tpack, spack):
        pack[64:72] = geo_rows
        pack[72:80] = own_rows
    for c in copies[:2]:
        c.wait()


def tile_place(n_j):
    return lambda t: ((t // n_j) * TI, lax.rem(t, n_j) * TJ)


def own_kernel(
    geo_ref, adj, fwd, near,
    right, rightn, xj_ref, fcol, tsum, ssum,
    left, xi_ref, frow, prod, abc,
):
    width = geo_ref.shape[1]
    geo = geo_ref[...]
    center = center_of(geo)
    first, second = pl.ds(0, width), pl.ds(width, width)
    build_targets(geo, adj[...], center, first, left, xi_ref, frow)
    build_sources(geo, fwd[...], center, first, right, rightn, xj_ref, fcol)
    build_sources(near[64:71], near[0:64], center, second, right, rightn, xj_ref, fcol)
    tsum[...] = jnp.zeros_like(tsum)
    ssum[...] = jnp.zeros_like(ssum)
    n_j = 2 * width // TJ
    run_tiles(
        (width // TI) * n_j, tile_place(n_j),
        left, right, rightn, xi_ref, xj_ref, frow, fcol, prod, abc, tsum, ssum,
    )


def reverse_bits(x, bits):
    out = jnp.zeros_like(x)
    for b in range(bits):
        out = out | (((x >> b) & 1) << (bits - 1 - b))
    return out


def rest_kernel(
    tpack, far, near, right, rightn, xj_ref, fcol, tsum_o, ssum_o,
    out_ref,
    left, xi_ref, frow, prod, abc, tsum, ssum,
):
    width = tpack.shape[1]
    geo, geo_s = tpack[64:71], near[64:71]
    center = center_of(geo)
    first, second = pl.ds(0, width), pl.ds(width, width)
    tsum[...] = jnp.zeros_like(tsum)
    ssum[...] = ssum_o[...]
    build_targets(far[64:71], far[0:64], center, first, left, xi_ref, frow)
    n_j = 2 * width // TJ
    run_tiles(
        (width // TI) * n_j, tile_place(n_j),
        left, right, rightn, xi_ref, xj_ref, frow, fcol, prod, abc, tsum, ssum,
    )

    def target_grad(g, acc):
        x = (g[0:3] - center) * TURNS
        m = g[3:6] * (1.0 / WAVENUM)
        sb, an, sc = read_sums(acc)
        gx = (2.0 * math.pi) * (x * sc[3:4] - sc[0:3]) + an - m * sb[3:4]
        gn = sb[0:3] - x * sb[3:4]
        return gx * TURNS, gn * (1.0 / WAVENUM)

    def source_grad(g, cols):
        x = (g[0:3] - center) * TURNS
        n = g[3:6]
        sa, bm, sc = read_sums(ssum[:, cols])
        gx = (2.0 * math.pi) * (x * sc[3:4] - sc[0:3]) - n * sa[3:4] + bm
        gn = sa[0:3] - x * sa[3:4]
        return gx * TURNS, gn

    t_own, s_own = target_grad(geo, tsum_o[...]), source_grad(geo, first)
    zero2 = jnp.zeros((2, width), F32)
    grads = [
        (t_own[0] + s_own[0], t_own[1] + s_own[1]),
        target_grad(far[64:71], tsum[...]),
        source_grad(geo_s, second),
    ]
    slots, _, cp_dev = out_ref.shape
    low_iota = lax.broadcasted_iota(jnp.int32, (2 * cp_dev, width), 0)
    terms = []
    for (gx, gn), rows in zip(grads, (tpack[72:80], far[72:80], near[72:80])):
        own_of, wt_of = rows[4:8].astype(jnp.int32), rows[0:4]
        g = jnp.concatenate([gx, gn, zero2], axis=0)
        place_of = reverse_bits(own_of // cp_dev, slots.bit_length() - 1)
        low = lax.rem(own_of, cp_dev) + (place_of & 1) * cp_dev
        place_of = place_of >> 1
        for s in range(4):
            gw = g * wt_of[s : s + 1]
            hi = hi_part(gw)
            here = jnp.where(low[s : s + 1] == low_iota, 1.0, 0.0).astype(BF16)
            both = jnp.concatenate([hi, gw - hi], axis=0).astype(BF16)
            where_to = jnp.broadcast_to(place_of[s : s + 1].astype(F32), both.shape).astype(BF16)
            terms.append((where_to, both, here))
    onehot = jnp.concatenate([t[2] for t in terms], axis=1)
    where_to = jnp.concatenate([t[0] for t in terms], axis=1)
    both = jnp.concatenate([t[1] for t in terms], axis=1)

    def add_owner(s0):
        rows = [jnp.where(where_to == (s0 // 2 + r), both, jnp.zeros_like(both)) for r in range(8)]
        acc = dot(jnp.concatenate(rows, axis=0), onehot, NT).reshape(8, 16, 2 * cp_dev)
        acc = acc[:, 0:8] + acc[:, 8:16]
        for r in range(8):
            out_ref[s0 + 2 * r] = acc[r, :, 0:cp_dev]
            out_ref[s0 + 2 * r + 1] = acc[r, :, cp_dev:]

    for s0 in range(0, slots, 16):
        add_owner(s0)


def shape(dims, kind):
    return jax.ShapeDtypeStruct(dims, kind)


def tile_scratch():
    return [pltpu.VMEM((2, 4, TI, TJ), F32), pltpu.VMEM((2, 5, TI, TJ), BF16)]


PARAMS = pltpu.CompilerParams(vmem_limit_bytes=20 * 1024 * 1024)


def pack_call(geo, adj, fwd, own, wt):
    width = geo.shape[1]
    return pl.pallas_call(
        pack_kernel,
        in_specs=[pl.BlockSpec(memory_space=pl.ANY)] * 5,
        out_shape=[shape((80, width), F32)] * 2,
        scratch_shapes=[
            pltpu.VMEM((7, width), F32), pltpu.VMEM((4, width), jnp.int32), pltpu.VMEM((4, width), F32),
            pltpu.SemaphoreType.DMA((5,)),
        ],
        name="pack",
    )(geo, adj, fwd, own, wt)


def target_scratch(width):
    return [
        pltpu.VMEM((width, 256), BF16), pltpu.VMEM((3, width, LANE), F32), pltpu.VMEM((3, 32, width), BF16)
    ] + tile_scratch()


def own_call(args):
    width = args[0].shape[1]
    total = 2 * width
    return pl.pallas_call(
        own_kernel,
        out_shape=[
            shape((2, 256, total), BF16), shape((2, 128, total), BF16), shape((8, total), F32),
            shape((3, 32, total), BF16), shape((32, width), F32), shape((32, total), F32),
        ],
        scratch_shapes=target_scratch(width),
        compiler_params=PARAMS,
        cost_estimate=pl.CostEstimate(flops=8 * 10**9, bytes_accessed=4 * 10**6, transcendentals=0),
        name="own",
    )(*args)


def rest_call(args, slots, cp_dev):
    width = args[0].shape[1]
    return pl.pallas_call(
        rest_kernel,
        out_shape=shape((slots, 8, cp_dev), F32),
        scratch_shapes=target_scratch(width) + [pltpu.VMEM((32, width), F32), pltpu.VMEM((32, 2 * width), F32)],
        compiler_params=PARAMS,
        cost_estimate=pl.CostEstimate(flops=8 * 10**9, bytes_accessed=4 * 10**6, transcendentals=0),
        name="rest",
    )(*args)


def swap(x, axis, bit):
    size = lax.axis_size(axis)
    return lax.ppermute(x, axis, [(k, k ^ bit) for k in range(size)])


def halving(cur):
    n_loop = lax.axis_size("loop").bit_length() - 1
    n_row = lax.axis_size("row").bit_length() - 1
    steps = [("loop", 1 << b) for b in range(n_loop)] + [("row", 1 << b) for b in range(n_row)]
    for axis, bit in steps:
        half = cur.shape[0] // 2
        up = jnp.where((lax.axis_index(axis) & bit) > 0, 1, 0)
        keep = lax.dynamic_slice_in_dim(cur, up * half, half, 0)
        send = lax.dynamic_slice_in_dim(cur, (1 - up) * half, half, 0)
        cur = keep + swap(send, axis, bit)
    return cur[0, 0:6]


def on_device(cp_dev, geometry, adjoint, forward, owner_map, owner_weight):
    slots = lax.axis_size("row") * lax.axis_size("loop")
    tpack, spack = pack_call(geometry, adjoint, forward, owner_map, owner_weight)
    near = swap(spack, "loop", 1)
    far = swap(tpack, "loop", 2)
    tables = own_call((geometry, adjoint, forward, near))
    return halving(rest_call((tpack, far, near, *tables), slots, cp_dev))


def solution(mesh):
    spec = P(None, ("parts", "row", "loop"))
    return jax.shard_map(
        functools.partial(on_device, 32), mesh=mesh, in_specs=(spec,) * 5, out_specs=spec, check_vma=False
    )
```

```python
import functools
import math

import jax
import jax.numpy as jnp
from jax import lax
from jax.experimental import pallas as pl
from jax.experimental.pallas import tpu as pltpu
from jax.sharding import PartitionSpec as P

WAVENUM = 2.0 * math.pi * 6000.0 / 1500.0
TURNS = WAVENUM / (2.0 * math.pi)
PAIR_SCALE = WAVENUM**3 / (4.0 * math.pi * TURNS)
F32 = jnp.float32
BF16 = jnp.bfloat16
TI = 256
TJ = 256
SUB = 16
STEP = 8
LAST = 32
LAST_STEP = 16
LANE = 128
WIDE = 256


def _fit(fn, odd, terms):
    import numpy as np

    nodes = 0.5 * np.cos(np.pi * (np.arange(400) + 0.5) / 400)
    cols = np.stack([nodes ** (2 * n + odd) for n in range(terms)], axis=1)
    coef = np.linalg.lstsq(cols, fn(nodes), rcond=None)[0]
    return [float(np.float32(c)) for c in coef]


def _sine():
    import numpy as np

    return _fit(lambda t: math.sqrt(2.0) * np.sin(np.pi * t), 1, 5)


SIN_C = _sine()


def horner(coef, y):
    acc = coef[-1] * y + coef[-2]
    for c in coef[-3::-1]:
        acc = acc * y + c
    return acc


def hi_part(x):
    return x.astype(BF16).astype(F32)


def split3(x):
    one = hi_part(x)
    rest = x - one
    two = hi_part(rest)
    return one, two, rest - two


SPLIT_PAIRS = ((0, 0), (0, 1), (1, 0), (0, 2), (2, 0), (1, 1), (1, 2), (2, 1))


def rows8(x, n, a, b):
    return jnp.concatenate([x, n, a, b], axis=0)


def target_rows(geo, center):
    x = (geo[0:3] - center) * TURNS
    m = geo[3:6] * (1.0 / WAVENUM)
    ones = jnp.ones_like(x[0:1])
    xm = jnp.sum(x * m, axis=0, keepdims=True)
    return x, m, split3(rows8(x, m, ones, xm))


def target_table(adj, rows):
    hi = hi_part(adj)
    lo = adj - hi
    return jnp.concatenate([rows[a] for a, _ in SPLIT_PAIRS] + [hi, hi, lo], axis=0)


def source_rows(geo, center):
    x = (geo[0:3] - center) * TURNS
    n = geo[3:6]
    return x, n


def source_table(geo, fwd, x, n):
    area = geo[6:7]
    scaled = fwd * (area * PAIR_SCALE)
    re, im = scaled[0:32], scaled[32:64]
    real = jnp.concatenate([re, im], axis=0)
    imag = jnp.concatenate([im, -re], axis=0)
    rh, ih = hi_part(real), hi_part(imag)
    zero3 = jnp.zeros_like(x)
    zero1 = jnp.zeros_like(x[0:1])
    ones = jnp.ones_like(zero1)
    xn = jnp.sum(x * n, axis=0, keepdims=True)
    prow = split3(rows8(-n, zero3, xn, zero1))
    qrow = split3(rows8(zero3, -x, zero1, ones))
    zeros = jnp.zeros((64, x.shape[1]), F32)
    cols = [
        jnp.concatenate([zeros, rh, real - rh, rh], axis=0),
        jnp.concatenate([zeros, ih, imag - ih, ih], axis=0),
        jnp.concatenate([prow[b] for _, b in SPLIT_PAIRS] + [zeros], axis=0),
        jnp.concatenate([qrow[b] for _, b in SPLIT_PAIRS] + [zeros], axis=0),
    ]
    return cols


def pair_chunk(prod, xi, xj, area):
    wr, wi, pn, q = prod
    d0, d1, d2 = xi[0] - xj[0], xi[1] - xj[1], xi[2] - xj[2]
    r2 = (d0 * d0 + d1 * d1) + (d2 * d2 + area)
    rs = lax.rsqrt(r2)
    turns = r2 * rs
    t = turns - jnp.round(turns)
    v = rs * (1.0 / (2.0 * math.pi))
    y = t * t
    sv = (t * v) * horner(SIN_C, y)
    v2 = v * v
    ec = v2 - sv * sv
    cv2 = jnp.maximum(v2 + ec, 1e-30)
    es = (sv * cv2) * lax.rsqrt(cv2)
    yr = ec * wr - es * wi
    yi = ec * wi + es * wr
    a = yi + v * yr
    b = yr - v * yi
    c = rs * ((q * yi - pn * yr) + (3.0 * v) * (pn * a + q * b))
    return a, b, c


def dot(a, b, dims=(((1,), (0,)), ((), ()))):
    return lax.dot_general(a, b, dims, preferred_element_type=F32)


def sum_splits(x):
    return x[0:8] + x[8:16] + x[16:24]


NT = (((1,), (1,)), ((), ()))


def sum_rows(x, n):
    width = x.shape[1]
    zero = jnp.zeros((1, width), F32)
    x1, x2, x3 = split3(x)
    n1 = hi_part(n)
    xr = jnp.concatenate([x1, jnp.ones_like(zero), x2, zero, x3, zero], axis=0)
    nr = jnp.concatenate([n1, zero, n - n1, zero], axis=0)
    z12, z20 = jnp.zeros((12, width), F32), jnp.zeros((20, width), F32)
    rows = ([xr, z20], [z12, nr, z12], [z20, xr])
    return [jnp.concatenate(r, axis=0).astype(BF16) for r in rows]


def read_sums(acc):
    return acc[0:4] + acc[4:8] + acc[8:12], acc[12:15] + acc[16:19], acc[20:24] + acc[24:28] + acc[28:32]


def build_targets(geo, adj, center, cols, left, xi_ref, frow):
    x, m, rows = target_rows(geo, center)
    left[cols, :] = target_table(adj, rows).T.astype(BF16)
    sums = sum_rows(x, m)
    for k in range(3):
        frow[k, :, cols] = sums[k]
    xt = jnp.concatenate([x, m, m[0:2]], axis=0).T
    for k in range(3):
        xi_ref[k, cols, :] = jnp.broadcast_to(xt[:, k : k + 1], (x.shape[1], LANE))


def build_sources(geo, fwd, center, cols, right, rightn, xj_ref, fcol):
    x, n = source_rows(geo, center)
    xj_ref[:, cols] = jnp.concatenate([x, geo[6:7] * (TURNS * TURNS)] * 2, axis=0)
    tab = source_table(geo, fwd, x, n)
    for k in range(2):
        right[k, :, cols] = tab[k].astype(BF16)
        rightn[k, :, cols] = tab[k + 2].astype(BF16)
    sums = sum_rows(x, n)
    for k, part in enumerate((sums[1], sums[0], sums[2])):
        fcol[k, :, cols] = part


def center_of(geo):
    return jnp.round(jnp.mean(geo[0:3], axis=1, keepdims=True))


def run_tiles(count, place, left, right, rightn, xi_ref, xj_ref, frow, fcol, prod, abc, tsum, ssum):
    def start(t):
        i0, j0 = place(t)
        return pl.multiple_of(i0, TI), pl.multiple_of(j0, TJ)

    def products(t, slot):
        i0, j0 = start(t)

        def piece(k):
            if k < 2:
                prod[slot, k] = dot(left[pl.ds(i0, TI), :], right[k, :, pl.ds(j0, TJ)])
            else:
                prod[slot, k] = dot(left[pl.ds(i0, TI), 0:128], rightn[k - 2, :, pl.ds(j0, TJ)])

        return [functools.partial(piece, k) for k in range(4)]

    def values(t, slot):
        i0, j0 = start(t)

        def piece(jj, top, size, step):
            here = slice(jj * WIDE, (jj + 1) * WIDE)
            xj = [xj_ref[k : k + 1, pl.ds(j0 + jj * WIDE, WIDE)] for k in range(4)]
            rows = pl.ds(top, size)
            bands = []
            for r in range(top, top + size, step):
                xi = [xi_ref[k, pl.ds(i0 + r, step), :] for k in range(3)]
                xi = [jnp.concatenate([v, v], axis=1) for v in xi]
                pr = [prod[slot, k, pl.ds(r, step), here] for k in range(4)]
                bands.append(pair_chunk(pr, xi, xj[0:3], xj[3]))
            a, b, c = [jnp.concatenate(parts, axis=0) for parts in zip(*bands)]
            for k, val in ((0, a), (2, c)):
                hi = val.astype(BF16)
                abc[slot, k, rows, here] = hi
                abc[slot, k + 1, rows, here] = (val - hi.astype(F32)).astype(BF16)
            abc[slot, 4, rows, here] = b.astype(BF16)

        todo = [(jj, top, SUB, STEP) for jj in range(TJ // WIDE) for top in range(0, TI, SUB)]
        if LAST > SUB:
            todo = todo[: -(LAST // SUB)] + [(TJ // WIDE - 1, TI - LAST, LAST, LAST_STEP)]
        return [functools.partial(piece, *args) for args in todo]

    def sums(t, slot, grouped=False):
        i0, j0 = start(t)
        kept = [None, None]
        groups = ((0, (0,)), (0, (1,)), (2, (2,)), (2, (3,)), (1, (4,)))
        if grouped:
            groups = ((0, (0, 1)), (2, (2, 3)), (1, (4,)))

        def piece(n, k, parts):
            fi = frow[k, :, pl.ds(i0, TI)]
            add = dot(
                jnp.concatenate([fi] * len(parts), axis=1),
                jnp.concatenate([abc[slot, p] for p in parts], axis=0),
            )
            kept[0] = add if n == 0 else kept[0] + add
            if n == len(groups) - 1:
                ssum[:, pl.ds(j0, TJ)] += kept[0]

        def other(n, k, parts):
            fj = fcol[k, :, pl.ds(j0, TJ)]
            add = dot(
                jnp.concatenate([fj] * len(parts), axis=1),
                jnp.concatenate([abc[slot, p] for p in parts], axis=1),
                NT,
            )
            kept[1] = add if n == 0 else kept[1] + add
            if n == len(groups) - 1:
                tsum[:, pl.ds(i0, TI)] += kept[1]

        return [functools.partial(f, n, *g) for n, g in enumerate(groups) for f in (piece, other)]

    def interleave(vector, matrix):
        done = 0
        for n, todo in enumerate(vector):
            while done < len(matrix) and done * len(vector) <= n * len(matrix):
                matrix[done]()
                done += 1
            todo()
        for rest in matrix[done:]:
            rest()

    last = count - 1
    for todo in products(0, 0):
        todo()
    abc[1] = jnp.zeros_like(abc[1])

    def double(u, _):
        t = 2 * u
        def half(h, _):
            @pl.when(h == 0)
            def _():
                interleave(values(t, 0), products(t + 1, 1) + sums(jnp.maximum(t - 1, 0), 1))

            @pl.when(h == 1)
            def _():
                interleave(values(t + 1, 1), products(jnp.minimum(t + 2, last), 0) + sums(t, 0))

            return 0

        lax.fori_loop(0, 2, half, 0)
        return 0

    lax.fori_loop(0, count // 2, double, 0)
    for todo in sums(last, 1, True):
        todo()


def pack_kernel(geo, adj, fwd, own, wt, tpack, spack, geo_v, own_v, wt_v, sems):
    copies = [
        pltpu.make_async_copy(src, dst, sems.at[k])
        for k, (src, dst) in enumerate(
            ((adj, tpack.at[0:64]), (fwd, spack.at[0:64]), (geo, geo_v), (own, own_v), (wt, wt_v))
        )
    ]
    for c in copies:
        c.start()
    for c in copies[2:]:
        c.wait()
    geo_rows = jnp.concatenate([geo_v[...], jnp.zeros_like(geo_v[0:1])], axis=0)
    own_rows = jnp.concatenate([wt_v[...], own_v[...].astype(F32)], axis=0)
    for pack in (tpack, spack):
        pack[64:72] = geo_rows
        pack[72:80] = own_rows
    for c in copies[:2]:
        c.wait()


def tile_place(n_j):
    return lambda t: ((t // n_j) * TI, lax.rem(t, n_j) * TJ)


def own_kernel(
    geo_ref, adj, fwd, near,
    right, rightn, xj_ref, fcol, tsum, ssum,
    left, xi_ref, frow, prod, abc,
):
    width = geo_ref.shape[1]
    geo = geo_ref[...]
    center = center_of(geo)
    first, second = pl.ds(0, width), pl.ds(width, width)
    build_targets(geo, adj[...], center, first, left, xi_ref, frow)
    build_sources(geo, fwd[...], center, first, right, rightn, xj_ref, fcol)
    build_sources(near[64:71], near[0:64], center, second, right, rightn, xj_ref, fcol)
    tsum[...] = jnp.zeros_like(tsum)
    ssum[...] = jnp.zeros_like(ssum)
    n_j = 2 * width // TJ
    run_tiles(
        (width // TI) * n_j, tile_place(n_j),
        left, right, rightn, xi_ref, xj_ref, frow, fcol, prod, abc, tsum, ssum,
    )


def reverse_bits(x, bits):
    out = jnp.zeros_like(x)
    for b in range(bits):
        out = out | (((x >> b) & 1) << (bits - 1 - b))
    return out


def rest_kernel(
    tpack, far, near, right, rightn, xj_ref, fcol, tsum_o, ssum_o,
    out_ref,
    left, xi_ref, frow, prod, abc, tsum, ssum,
):
    width = tpack.shape[1]
    geo, geo_s = tpack[64:71], near[64:71]
    center = center_of(geo)
    first, second = pl.ds(0, width), pl.ds(width, width)
    tsum[...] = jnp.zeros_like(tsum)
    ssum[...] = ssum_o[...]
    build_targets(far[64:71], far[0:64], center, first, left, xi_ref, frow)
    n_j = 2 * width // TJ
    run_tiles(
        (width // TI) * n_j, tile_place(n_j),
        left, right, rightn, xi_ref, xj_ref, frow, fcol, prod, abc, tsum, ssum,
    )

    def target_grad(g, acc):
        x = (g[0:3] - center) * TURNS
        m = g[3:6] * (1.0 / WAVENUM)
        sb, an, sc = read_sums(acc)
        gx = (2.0 * math.pi) * (x * sc[3:4] - sc[0:3]) + an - m * sb[3:4]
        gn = sb[0:3] - x * sb[3:4]
        return gx * TURNS, gn * (1.0 / WAVENUM)

    def source_grad(g, cols):
        x = (g[0:3] - center) * TURNS
        n = g[3:6]
        sa, bm, sc = read_sums(ssum[:, cols])
        gx = (2.0 * math.pi) * (x * sc[3:4] - sc[0:3]) - n * sa[3:4] + bm
        gn = sa[0:3] - x * sa[3:4]
        return gx * TURNS, gn

    t_own, s_own = target_grad(geo, tsum_o[...]), source_grad(geo, first)
    zero2 = jnp.zeros((2, width), F32)
    grads = [
        (t_own[0] + s_own[0], t_own[1] + s_own[1]),
        target_grad(far[64:71], tsum[...]),
        source_grad(geo_s, second),
    ]
    slots, _, cp_dev = out_ref.shape
    low_iota = lax.broadcasted_iota(jnp.int32, (2 * cp_dev, width), 0)
    terms = []
    for (gx, gn), rows in zip(grads, (tpack[72:80], far[72:80], near[72:80])):
        own_of, wt_of = rows[4:8].astype(jnp.int32), rows[0:4]
        g = jnp.concatenate([gx, gn, zero2], axis=0)
        place_of = reverse_bits(own_of // cp_dev, slots.bit_length() - 1)
        low = lax.rem(own_of, cp_dev) + (place_of & 1) * cp_dev
        place_of = place_of >> 1
        for s in range(4):
            gw = g * wt_of[s : s + 1]
            hi = hi_part(gw)
            here = jnp.where(low[s : s + 1] == low_iota, 1.0, 0.0).astype(BF16)
            both = jnp.concatenate([hi, gw - hi], axis=0).astype(BF16)
            where_to = jnp.broadcast_to(place_of[s : s + 1].astype(F32), both.shape).astype(BF16)
            terms.append((where_to, both, here))
    onehot = jnp.concatenate([t[2] for t in terms], axis=1)
    where_to = jnp.concatenate([t[0] for t in terms], axis=1)
    both = jnp.concatenate([t[1] for t in terms], axis=1)

    def add_owner(s0):
        rows = [jnp.where(where_to == (s0 // 2 + r), both, jnp.zeros_like(both)) for r in range(8)]
        acc = dot(jnp.concatenate(rows, axis=0), onehot, NT).reshape(8, 16, 2 * cp_dev)
        acc = acc[:, 0:8] + acc[:, 8:16]
        for r in range(8):
            out_ref[s0 + 2 * r] = acc[r, :, 0:cp_dev]
            out_ref[s0 + 2 * r + 1] = acc[r, :, cp_dev:]

    for s0 in range(0, slots, 16):
        add_owner(s0)


def shape(dims, kind):
    return jax.ShapeDtypeStruct(dims, kind)


def tile_scratch():
    return [pltpu.VMEM((2, 4, TI, TJ), F32), pltpu.VMEM((2, 5, TI, TJ), BF16)]


PARAMS = pltpu.CompilerParams(vmem_limit_bytes=20 * 1024 * 1024)


def pack_call(geo, adj, fwd, own, wt):
    width = geo.shape[1]
    return pl.pallas_call(
        pack_kernel,
        in_specs=[pl.BlockSpec(memory_space=pl.ANY)] * 5,
        out_shape=[shape((80, width), F32)] * 2,
        scratch_shapes=[
            pltpu.VMEM((7, width), F32), pltpu.VMEM((4, width), jnp.int32), pltpu.VMEM((4, width), F32),
            pltpu.SemaphoreType.DMA((5,)),
        ],
        name="pack",
    )(geo, adj, fwd, own, wt)


def target_scratch(width):
    return [
        pltpu.VMEM((width, 256), BF16), pltpu.VMEM((3, width, LANE), F32), pltpu.VMEM((3, 32, width), BF16)
    ] + tile_scratch()


def own_call(args):
    width = args[0].shape[1]
    total = 2 * width
    return pl.pallas_call(
        own_kernel,
        out_shape=[
            shape((2, 256, total), BF16), shape((2, 128, total), BF16), shape((8, total), F32),
            shape((3, 32, total), BF16), shape((32, width), F32), shape((32, total), F32),
        ],
        scratch_shapes=target_scratch(width),
        compiler_params=PARAMS,
        cost_estimate=pl.CostEstimate(flops=8 * 10**9, bytes_accessed=4 * 10**6, transcendentals=0),
        name="own",
    )(*args)


def rest_call(args, slots, cp_dev):
    width = args[0].shape[1]
    return pl.pallas_call(
        rest_kernel,
        out_shape=shape((slots, 8, cp_dev), F32),
        scratch_shapes=target_scratch(width) + [pltpu.VMEM((32, width), F32), pltpu.VMEM((32, 2 * width), F32)],
        compiler_params=PARAMS,
        cost_estimate=pl.CostEstimate(flops=8 * 10**9, bytes_accessed=4 * 10**6, transcendentals=0),
        name="rest",
    )(*args)


def swap(x, axis, bit):
    size = lax.axis_size(axis)
    return lax.ppermute(x, axis, [(k, k ^ bit) for k in range(size)])


def halving(cur):
    n_loop = lax.axis_size("loop").bit_length() - 1
    n_row = lax.axis_size("row").bit_length() - 1
    steps = [("loop", 1 << b) for b in range(n_loop)] + [("row", 1 << b) for b in range(n_row)]
    for axis, bit in steps:
        half = cur.shape[0] // 2
        up = jnp.where((lax.axis_index(axis) & bit) > 0, 1, 0)
        keep = lax.dynamic_slice_in_dim(cur, up * half, half, 0)
        send = lax.dynamic_slice_in_dim(cur, (1 - up) * half, half, 0)
        cur = keep + swap(send, axis, bit)
    return cur[0, 0:6]


def on_device(cp_dev, geometry, adjoint, forward, owner_map, owner_weight):
    slots = lax.axis_size("row") * lax.axis_size("loop")
    tpack, spack = pack_call(geometry, adjoint, forward, owner_map, owner_weight)
    near = swap(spack, "loop", 1)
    far = swap(tpack, "loop", 2)
    tables = own_call((geometry, adjoint, forward, near))
    return halving(rest_call((tpack, far, near, *tables), slots, cp_dev))


def solution(mesh):
    spec = P(None, ("parts", "row", "loop"))
    return jax.shard_map(
        functools.partial(on_device, 32), mesh=mesh, in_specs=(spec,) * 5, out_specs=spec, check_vma=False
    )
```
